128 devices in a mesh: seq: 16 (over y, z), head: 8 (over x, core).
Axes of the slice: x: 4, y: 4, z: 4, core: 2. Of those that a mesh axis runs over, the one named last changes fastest.
Arguments:
- query_rows: bfloat16 [32768, 4096], P('seq', 'head'), may hold values from -6 to 6
- key_rows: bfloat16 [32768, 4096], P('seq', 'head'), may hold values from -6 to 6
- value_rows: bfloat16 [32768, 4096], P('seq', 'head'), may hold values from -6 to 6
- out_cotangent: bfloat16 [32768, 4096], P('seq', 'head'), may hold values from -6 to 6
- norm_gain: float32 [4096], P('head'), may hold values from 0.5 to 1.5
- decay_rate: float32 [32], P('head'), may hold values from 6.1035156e-06 to 0.0333333333
- document_lengths: int32 [32], replicated, may hold values from 1 to 16384, 32768 in all
- group_home: int32 [256], P('seq'), may hold values from 0 to 255, as said below
Outputs:
- query_grad: bfloat16 [32768, 4096], P('seq', 'head')
- key_grad: bfloat16 [32768, 4096], P('seq', 'head')
- value_grad: bfloat16 [32768, 4096], P('seq', 'head')
The draws below stay inside these ranges and needn't reach their ends.
Inputs may be any that keep to these rules, and one draw needn't show every extreme that they name: document_lengths sum to 32768; the longest holds exactly half of them. group_home is a permutation of the 256 sequence groups; the groups stored on one device along seq hold exactly one group of each device's aligned block of sequence groups.
All inputs are finite; a program needn't handle non-finite values.
Results may differ from the reference program's by a relative error of at most 0.0095.
Values may be sent and summed in bfloat16 or wider, within the bound.
A program may use at most 128 MiB of HBM per device.

```python
import math
import jax
import jax.numpy as jnp
import numpy as np
from jax import lax

HEAD_SIZE = 128
SPAN = 256
DOCS = 32
TOK_DEV = 2048
TOKENS = 32768
SPANS = 128
GROUP = 128
GROUPS = 256
HEADS = 32
CHANNELS = 4096


def draw_decay_rate(key, part):
    pick_key, fast_key, slow_key = jax.random.split(key, 3)
    slow_share = 0.5
    slow_heads = jax.random.uniform(pick_key, (HEADS,)) < slow_share
    fast_rate = jnp.exp(jax.random.uniform(fast_key, (HEADS,), minval=jnp.log(1.0 / 50.0), maxval=jnp.log(1.0 / 30.0)))
    slow_rate = jnp.exp(jax.random.uniform(slow_key, (HEADS,), minval=jnp.log(0.2 / TOKENS), maxval=jnp.log(2.0 / TOKENS)))
    return jnp.where(slow_heads, slow_rate, fast_rate).astype(jnp.float32)


def draw_group_home(key, part):
    devices = TOK_DEV // GROUP
    offset_key, source_key, target_key = jax.random.split(key, 3)
    shifts = jax.random.permutation(offset_key, devices)
    source_order = jax.vmap(lambda row_key: jax.random.permutation(row_key, devices))(jax.random.split(source_key, devices))
    target_order = jax.vmap(lambda row_key: jax.random.permutation(row_key, devices))(jax.random.split(target_key, devices))
    sources = jnp.arange(devices, dtype=jnp.int32)[:, None]
    targets = (sources + shifts[None, :]) % devices
    stored = sources * devices + source_order
    sources_full = jnp.broadcast_to(sources, targets.shape)
    home = targets * devices + target_order[targets, sources_full]
    return jnp.zeros((GROUPS,), jnp.int32).at[stored.reshape(-1)].set(home.reshape(-1).astype(jnp.int32))


def block_scale(key, extent, cuts, low, high):
    factor_of = 1.0
    for dim, parts in cuts:
        draws = jax.random.uniform(jax.random.fold_in(jax.random.fold_in(key, 6), dim), (parts,), jnp.float32, low / len(cuts), high / len(cuts))
        factor_of = factor_of * jnp.repeat(jnp.exp(draws), extent[dim] // parts).reshape((-1,) + (1,) * (len(extent) - 1 - dim))
    return factor_of


def length_profile(count, total, most, skew):
    loads = [(1 << 20) // math.isqrt(standing ** skew) + 1 for standing in range(2, count + 1)]
    surplus, given = total - most - (count - 1), [1] * (count - 1)
    while surplus > 0:
        candidates = [i for i in range(count - 1) if given[i] < most]
        pool, left = sum([loads[i] for i in candidates]), surplus
        for i in candidates:
            addition = min(most - given[i], max(1, left * loads[i] // pool), surplus)
            given[i] = given[i] + addition
            surplus = surplus - addition
    return np.array([most] + given)


def ragged_sizes(own_key, number_of, total, limit, skew):
    if number_of == 2:
        one = jax.random.randint(own_key, (), max(1, total - limit), min(limit, total - 1) + 1)
        return jnp.stack([one, total - one])
    sizes = jnp.asarray(length_profile(number_of, total, limit, skew), jnp.int32)
    twos = (number_of - 1) // 2
    giver, receiver = sizes[1:1 + 2 * twos:2], sizes[2:2 + 2 * twos:2]
    margin = jnp.minimum(giver - 1, limit - receiver)
    passed = jax.random.randint(jax.random.fold_in(own_key, 1), (twos,), 0, 1 << 20) % (margin + 1)
    sizes = sizes.at[1:1 + 2 * twos:2].set(giver - passed).at[2:2 + 2 * twos:2].set(receiver + passed)
    return sizes[jax.random.permutation(jax.random.fold_in(own_key, 2), number_of)]


def scatter_about(key, extent, deviation, limit, cuts=(), held_as=jnp.bfloat16):
    entries = jax.random.normal(key, extent, jnp.float32) * deviation
    if len(cuts) > 0:
        entries = block_scale(key, extent, cuts, -0.22, 0.18) * entries
    return jnp.clip(entries, min=-limit, max=limit).astype(held_as)


def setup_inputs(seed: int = 0) -> dict:
    key_of = jax.random.split(jax.random.key(seed), 9)
    return {
        "query_rows": scatter_about(key_of[0], (TOKENS, CHANNELS), 1.0, 6.0, ((0, 16), (1, 8))),
        "key_rows": scatter_about(key_of[1], (TOKENS, CHANNELS), 1.0, 6.0, ((0, 16), (1, 8))),
        "value_rows": scatter_about(key_of[2], (TOKENS, CHANNELS), 1.0, 6.0, ((0, 16), (1, 8))),
        "out_cotangent": scatter_about(key_of[3], (TOKENS, CHANNELS), 1.0, 6.0, ((0, 16), (1, 8))),
        "norm_gain": jnp.clip(1.0 + 0.1 * jax.random.normal(key_of[4], (CHANNELS,), jnp.float32), 0.5, 1.5),
        "decay_rate": draw_decay_rate(jax.random.fold_in(key_of[8], 71), 0),
        "document_lengths": ragged_sizes(key_of[6], DOCS, TOKENS, TOKENS // 2, 2).astype(jnp.int32),
        "group_home": draw_group_home(jax.random.fold_in(key_of[8], 71), 0),
    }


EPSILON = 1e-06

def segment_of(positions, doc_ends):
    return lax.optimization_barrier(jnp.sum((doc_ends <= positions[..., None]).astype(jnp.int32), axis=-1))

def span_weights(seq_spans, doc_ends, decay_rates, span_width):
    offsets = jnp.arange(span_width, dtype=jnp.int32)
    positions = seq_spans[:, None] * span_width + offsets[None, :]
    segment = segment_of(positions, doc_ends)
    before = jnp.where(seq_spans == 0, -1, segment_of(seq_spans * span_width - 1, doc_ends))
    last_segment = segment[:, -1]
    step_float = offsets.astype(jnp.float32)
    query_side = jnp.exp(-decay_rates[None, None, :] * (step_float[None, :, None] + 1.0)) * (segment == before[:, None]).astype(jnp.float32)[:, :, None]
    key_side = jnp.exp(-decay_rates[None, None, :] * (span_width - 1.0 - step_float)[None, :, None]) * (segment == last_segment[:, None]).astype(jnp.float32)[:, :, None]
    carry_rate = jnp.exp(-decay_rates * span_width)[None, :] * (before == last_segment).astype(jnp.float32)[:, None]
    return (query_side, key_side, carry_rate, segment)

def span_masks(segment, decay_rates, span_width):
    step_float = jnp.arange(span_width, dtype=jnp.float32)
    spread = step_float[:, None] - step_float[None, :]
    same_doc = (segment[:, :, None] == segment[:, None, :]) & (spread >= 0.0)[None]
    return jnp.where(same_doc[:, None], jnp.exp(-decay_rates[None, :, None, None] * jnp.maximum(spread, 0.0)[None, None]), 0.0)

def rounded(values):
    return lax.optimization_barrier(values.astype(jnp.bfloat16)).astype(jnp.float32)

def reference(query_rows, key_rows, value_rows, out_cotangent, norm_gain, decay_rate, document_lengths, group_home):
    doc_ends = jnp.cumsum(document_lengths).astype(jnp.int32)

    def to_sequence(stored):
        blocks = stored.reshape(GROUPS, GROUP, HEADS, HEAD_SIZE)
        ordered = jnp.zeros_like(blocks).at[group_home].set(blocks)
        return ordered.reshape(SPANS, SPAN, HEADS, HEAD_SIZE)
    query_seq = to_sequence(query_rows)
    key_seq = to_sequence(key_rows)
    value_seq = to_sequence(value_rows)
    upstream = to_sequence(out_cotangent)
    all_spans = jnp.arange(SPANS, dtype=jnp.int32)
    query_side, key_side, carry_rate, segment = span_weights(all_spans, doc_ends, decay_rate, SPAN)

    def forward_step(state, inputs):
        query_c, key_c, value_c, query_w, key_w, carry_c, segment_c = inputs
        decay_mask = span_masks(segment_c[None], decay_rate, SPAN)[0]
        query_f = query_c.astype(jnp.float32)
        key_f = key_c.astype(jnp.float32)
        value_f = value_c.astype(jnp.float32)
        prev_state = rounded(state)
        scores = jnp.einsum('jhd,lhd->hjl', query_f, key_f)
        mixing = rounded(scores * decay_mask)
        output = jnp.einsum('hjl,lhe->jhe', mixing, value_f) + query_w[..., None] * jnp.einsum('jhd,hde->jhe', query_f, prev_state)
        weighted = rounded(key_w[..., None] * value_f)
        summary = jnp.einsum('jhd,jhe->hde', key_f, weighted)
        return (carry_c[:, None, None] * state + summary, (output, prev_state))
    zero_state = jnp.zeros((HEADS, HEAD_SIZE, HEAD_SIZE), jnp.float32)
    _, (attn_out, prev_states) = lax.scan(forward_step, zero_state, (query_seq, key_seq, value_seq, query_side, key_side, carry_rate, segment))
    flat_out = attn_out.reshape(TOKENS, CHANNELS)
    upstream_f = upstream.reshape(TOKENS, CHANNELS).astype(jnp.float32)
    scaling = 1.0 / jnp.sqrt(lax.optimization_barrier(jnp.mean(flat_out * flat_out, axis=1)) + EPSILON)
    pulled = lax.optimization_barrier(jnp.mean(norm_gain * upstream_f * flat_out, axis=1))
    grad_in = (scaling[:, None] * norm_gain * upstream_f - (scaling ** 3)[:, None] * flat_out * pulled[:, None]).astype(jnp.bfloat16)
    grad_in = grad_in.reshape(SPANS, SPAN, HEADS, HEAD_SIZE)

    def backward_step(state, inputs):
        query_c, key_c, value_c, grad_c, query_w, key_w, carry_c, segment_c, prev_state = inputs
        decay_mask = span_masks(segment_c[None], decay_rate, SPAN)[0]
        query_f = query_c.astype(jnp.float32)
        key_f = key_c.astype(jnp.float32)
        value_f = value_c.astype(jnp.float32)
        grad_f = grad_c.astype(jnp.float32)
        after_state = rounded(state)
        mixing = rounded(jnp.einsum('jhd,lhd->hjl', query_f, key_f) * decay_mask)
        score_grad = rounded(jnp.einsum('jhe,lhe->hjl', grad_f, value_f) * decay_mask)
        query_grad = jnp.einsum('hjl,lhd->jhd', score_grad, key_f) + query_w[..., None] * jnp.einsum('jhe,hde->jhd', grad_f, prev_state)
        key_grad = jnp.einsum('hjl,jhd->lhd', score_grad, query_f) + key_w[..., None] * jnp.einsum('lhe,hde->lhd', value_f, after_state)
        value_grad = jnp.einsum('hjl,jhe->lhe', mixing, grad_f) + key_w[..., None] * jnp.einsum('lhd,hde->lhe', key_f, after_state)
        rev_summary = jnp.einsum('jhd,jhe->hde', query_f, rounded(query_w[..., None] * grad_f))
        return (rev_summary + carry_c[:, None, None] * state, (query_grad, key_grad, value_grad))
    _, (query_grad, key_grad, value_grad) = lax.scan(backward_step, zero_state, (query_seq, key_seq, value_seq, grad_in, query_side, key_side, carry_rate, segment, prev_states), reverse=True)

    def to_stored(values):
        blocks = values.reshape(GROUPS, GROUP, HEADS, HEAD_SIZE)
        return blocks[group_home].reshape(TOKENS, CHANNELS).astype(jnp.bfloat16)
    return (to_stored(query_grad), to_stored(key_grad), to_stored(value_grad))
```

```python
import functools

import jax
import jax.numpy as jnp
from jax import lax
from jax.experimental import pallas as pl
from jax.experimental.pallas import tpu as pltpu
from jax.sharding import PartitionSpec as P

HEAD = 128
GROUP = 128
RING = 4
EPSILON = 1e-06
MESH = pl.DeviceIdType.MESH
F32 = jnp.float32
BF16 = jnp.bfloat16


def dot(a, b, dims):
    return lax.dot_general(a, b, (dims, ((), ())), preferred_element_type=F32)


NN = ((1,), (0,))
NT = ((1,), (1,))
TN = ((0,), (0,))


def head_cols(h):
    return slice(h * HEAD, (h + 1) * HEAD)


def decay_tables(rate_ref, heads, dec_ref=None, qdec_ref=None, kdec_ref=None):
    row = lax.broadcasted_iota(jnp.int32, (GROUP, GROUP), 0).astype(F32)
    col = lax.broadcasted_iota(jnp.int32, (GROUP, GROUP), 1).astype(F32)
    for h in range(heads):
        r = rate_ref[h]
        if dec_ref is not None:
            spread = row - col
            dec_ref[h] = jnp.where(spread >= 0.0, jnp.exp(-r * jnp.maximum(spread, 0.0)), 0.0)
        if qdec_ref is not None:
            qdec_ref[h] = jnp.exp(-r * (row + 1.0))
        if kdec_ref is not None:
            kdec_ref[h] = jnp.exp(-r * (GROUP - 1.0 - row))


def seg_tiles(seg_ref):
    row = jnp.broadcast_to(seg_ref[0], (GROUP, GROUP))
    return row, row.T


def summary_kernel(heads, rate_ref, edge_ref, seg_ref, k_ref, v_ref, s_ref, kdec_ref):
    i = pl.program_id(0)

    @pl.when(i == 0)
    def _():
        decay_tables(rate_ref, heads, kdec_ref=kdec_ref)

    _, seg_c = seg_tiles(seg_ref)
    live = seg_c == edge_ref[1, i]
    for h in range(heads):
        side = jnp.where(live, kdec_ref[h], 0.0)
        weighted = (side * v_ref[:, head_cols(h)].astype(F32)).astype(BF16)
        s = dot(k_ref[:, head_cols(h)], weighted, TN).astype(BF16)
        s_ref[RING * h : RING * (h + 1), 0] = s.reshape(RING, HEAD // RING, HEAD)


def output_kernel(
    heads, rate_ref, edge_ref, seg_ref, q_ref, k_ref, v_ref, u_ref, p_ref, gain_ref,
    o_ref, sums_ref, dec_ref, qdec_ref,
):
    i = pl.program_id(0)

    @pl.when(i == 0)
    def _():
        decay_tables(rate_ref, heads, dec_ref=dec_ref, qdec_ref=qdec_ref)
        sums_ref[...] = jnp.zeros_like(sums_ref)

    seg_r, seg_c = seg_tiles(seg_ref)
    same = seg_r == seg_c
    live = seg_c == edge_ref[0, i]
    squares = jnp.zeros((GROUP, HEAD), F32)
    crossed = jnp.zeros((GROUP, HEAD), F32)
    for h in range(heads):
        cols = head_cols(h)
        q = q_ref[:, cols]
        mixing = (dot(q, k_ref[:, cols], NT) * jnp.where(same, dec_ref[h], 0.0)).astype(BF16)
        prev = p_ref[RING * h : RING * (h + 1), 0].reshape(HEAD, HEAD)
        out = dot(mixing, v_ref[:, cols], NN) + jnp.where(live, qdec_ref[h], 0.0) * dot(q, prev, NN)
        o_ref[:, cols] = out
        squares += out * out
        crossed += gain_ref[:, cols] * u_ref[:, cols].astype(F32) * out
    lane = lax.broadcasted_iota(jnp.int32, (GROUP, HEAD), 1)
    squares = jnp.sum(squares, axis=1, keepdims=True)
    crossed = jnp.sum(crossed, axis=1, keepdims=True)
    groups = pl.num_programs(0)
    sums_ref[...] += jnp.where(lane == i, squares, 0.0) + jnp.where(lane == i + groups, crossed, 0.0)


def cotangent_kernel(
    heads, channels, rate_ref, edge_ref, seg_ref, q_ref, u_ref, o_ref, gain_ref, sums_ref,
    g_ref, r_ref, qdec_ref,
):
    i = pl.program_id(0)

    @pl.when(i == 0)
    def _():
        decay_tables(rate_ref, heads, qdec_ref=qdec_ref)

    _, seg_c = seg_tiles(seg_ref)
    live = seg_c == edge_ref[0, i]
    lane = lax.broadcasted_iota(jnp.int32, (GROUP, HEAD), 1)
    groups = pl.num_programs(0)
    sums = sums_ref[...]
    squares = jnp.sum(jnp.where(lane == i, sums, 0.0), axis=1, keepdims=True)
    crossed = jnp.sum(jnp.where(lane == i + groups, sums, 0.0), axis=1, keepdims=True)
    scaling = lax.rsqrt(squares / channels + EPSILON)
    back = scaling * scaling * scaling * (crossed / channels)
    for h in range(heads):
        cols = head_cols(h)
        g = (scaling * (gain_ref[:, cols] * u_ref[:, cols].astype(F32)) - back * o_ref[:, cols]).astype(BF16)
        g_ref[:, cols] = g
        weighted = (jnp.where(live, qdec_ref[h], 0.0) * g.astype(F32)).astype(BF16)
        r = dot(q_ref[:, cols], weighted, TN).astype(BF16)
        r_ref[RING * h : RING * (h + 1), 0] = r.reshape(RING, HEAD // RING, HEAD)


def gradient_kernel(
    heads, rate_ref, edge_ref, seg_ref, q_ref, k_ref, v_ref, g_ref, p_ref, a_ref,
    qg_ref, kg_ref, vg_ref, dec_ref, qdec_ref, kdec_ref,
):
    i = pl.program_id(0)

    @pl.when(i == 0)
    def _():
        decay_tables(rate_ref, heads, dec_ref, qdec_ref, kdec_ref)

    seg_r, seg_c = seg_tiles(seg_ref)
    same = seg_r == seg_c
    live_q = seg_c == edge_ref[0, i]
    live_k = seg_c == edge_ref[1, i]
    for h in range(heads):
        cols = head_cols(h)
        q, k, v, g = q_ref[:, cols], k_ref[:, cols], v_ref[:, cols], g_ref[:, cols]
        prev = p_ref[RING * h : RING * (h + 1), 0].reshape(HEAD, HEAD)
        after = a_ref[RING * h : RING * (h + 1), 0].reshape(HEAD, HEAD)
        mask = jnp.where(same, dec_ref[h], 0.0)
        mixing = (dot(q, k, NT) * mask).astype(BF16)
        score = (dot(g, v, NT) * mask).astype(BF16)
        side_q = jnp.where(live_q, qdec_ref[h], 0.0)
        side_k = jnp.where(live_k, kdec_ref[h], 0.0)
        qg_ref[:, cols] = (dot(score, k, NN) + side_q * dot(g, prev, NT)).astype(BF16)
        kg_ref[:, cols] = (dot(score, q, TN) + side_k * dot(v, after, NT)).astype(BF16)
        vg_ref[:, cols] = (dot(mixing, g, TN) + side_k * dot(k, after, NN)).astype(BF16)


def torus_offsets(ring):
    offsets = [(dy, dz) for dy in range(ring) for dz in range(ring) if (dy, dz) != (0, 0)]
    return sorted(offsets, key=lambda o: min(o[0], ring - o[0]) + min(o[1], ring - o[1]))


def scan_kernel(
    ring, reverse, order_ref, home_ref, carry_ref, s_ref, p_ref,
    got_ref, seq_ref, back_ref, send1, recv1, send2, recv2, local_sem,
):
    me = lax.axis_index("seq")
    head = lax.axis_index("head")
    y, z = me // ring, lax.rem(me, ring)
    peers = [lax.rem(y + dy, ring) * ring + lax.rem(z + dz, ring) for dy, dz in torus_offsets(ring)]
    count = len(peers)
    per = got_ref.shape[0] // (count + 1)
    barrier = pltpu.get_barrier_semaphore()
    for peer in peers:
        pl.semaphore_signal(barrier, inc=1, device_id=(peer, head), device_id_type=MESH)
    own = pltpu.make_async_copy(s_ref.at[me], got_ref.at[pl.ds(me * per, per)], local_sem.at[0])
    own.start()
    pl.semaphore_wait(barrier, count)
    copies = []
    for n, peer in enumerate(peers):
        copy = pltpu.make_async_remote_copy(
            src_ref=s_ref.at[peer], dst_ref=got_ref.at[pl.ds(me * per, per)],
            send_sem=send1.at[n], recv_sem=recv1.at[n],
            device_id=(peer, head), device_id_type=MESH,
        )
        copy.start()
        copies.append(copy)
    own.wait()
    for copy in copies:
        copy.wait()
    groups = got_ref.shape[0]
    unroll = 8

    def step(b, state):
        for n in range(unroll):
            t = b * unroll + n
            if reverse:
                t = groups - 1 - t
            seq_ref[t] = state.astype(BF16)
            state = carry_ref[t] * state + got_ref[order_ref[t]].astype(F32)
        return state

    lax.fori_loop(0, groups // unroll, step, jnp.zeros(got_ref.shape[1:], F32))

    def put(b, _):
        for n in range(unroll):
            p = b * unroll + n
            back_ref[p] = seq_ref[home_ref[p]]
        return 0

    lax.fori_loop(0, groups // unroll, put, 0)
    own = pltpu.make_async_copy(back_ref.at[pl.ds(me * per, per)], p_ref.at[me], local_sem.at[1])
    own.start()
    copies = []
    for n, peer in enumerate(peers):
        copy = pltpu.make_async_remote_copy(
            src_ref=back_ref.at[pl.ds(peer * per, per)], dst_ref=p_ref.at[me],
            send_sem=send2.at[n], recv_sem=recv2.at[n],
            device_id=(peer, head), device_id_type=MESH,
        )
        copy.start()
        copies.append(copy)
    own.wait()
    for copy in copies:
        copy.wait()


def total_kernel(x_ref, o_ref, mine_ref, got_ref, send, recv):
    size = lax.axis_size("head")
    me = lax.axis_index("head")
    seq = lax.axis_index("seq")
    peers = [lax.rem(me + n, size) for n in range(1, size)]
    barrier = pltpu.get_barrier_semaphore()
    for peer in peers:
        pl.semaphore_signal(barrier, inc=1, device_id=(seq, peer), device_id_type=MESH)
    part = mine_ref.shape[0]
    packed = x_ref[0:part]
    for n in range(1, GROUP // part):
        packed = packed + pltpu.roll(x_ref[part * n : part * (n + 1)], n * part, 1)
    mine_ref[...] = packed
    pl.semaphore_wait(barrier, size - 1)
    copies = []
    for n, peer in enumerate(peers):
        copy = pltpu.make_async_remote_copy(
            src_ref=mine_ref, dst_ref=got_ref.at[n], send_sem=send.at[n], recv_sem=recv.at[n],
            device_id=(seq, peer), device_id_type=MESH,
        )
        copy.start()
        copies.append(copy)
    for copy in copies:
        copy.wait()
    total = mine_ref[...]
    for n in range(size - 1):
        total = total + got_ref[n]
    o_ref[0:part] = total
    for n in range(1, GROUP // part):
        o_ref[part * n : part * (n + 1)] = pltpu.roll(total, HEAD - n * part, 1)


def shards(q, k, v, u, gain, rate, lengths, home):
    devices = lax.axis_size("seq")
    sides = lax.axis_size("head")
    me = lax.axis_index("seq")
    heads = q.shape[1] // HEAD
    groups = home.shape[0]
    rows, width = q.shape
    docs = lengths.shape[0]
    ids = jnp.arange(docs, dtype=jnp.int32)
    ends = jnp.sum(jnp.where(ids[None, :] <= ids[:, None], lengths[None, :], 0), axis=1)

    def segment(pos):
        return jnp.sum((ends <= pos[..., None]).astype(jnp.int32), axis=-1)

    seg = segment(home[:, None] * GROUP + jnp.arange(GROUP, dtype=jnp.int32)[None, :]).astype(F32)
    before = jnp.where(home == 0, -1, segment(home * GROUP - 1)).astype(F32)
    last = segment(home * GROUP + GROUP - 1).astype(F32)
    edges = jnp.stack([before, last])
    seg = seg.reshape(groups, 1, GROUP)

    homes = lax.all_gather(home, "seq", tiled=True)
    total_groups = devices * groups
    steps = jnp.arange(total_groups, dtype=jnp.int32)
    order = jnp.sum(jnp.where(homes[None, :] == steps[:, None], steps[None, :], 0), axis=1)
    owner_head = me // RING
    own_rate = jnp.sum(jnp.where(jnp.arange(heads) == owner_head, rate, 0.0))
    joined = (steps == 0) | (segment(steps * GROUP - 1) == segment(steps * GROUP + GROUP - 1))
    carry = jnp.where(joined, jnp.exp(-own_rate * GROUP), 0.0)

    smem = pl.BlockSpec(memory_space=pltpu.SMEM)
    seg_spec = pl.BlockSpec((1, 1, GROUP), lambda i: (i, 0, 0))
    row_spec = pl.BlockSpec((GROUP, width), lambda i: (i, 0))
    state_spec = pl.BlockSpec((devices, 1, HEAD // RING, HEAD), lambda i: (0, i, 0, 0))
    gain_spec = pl.BlockSpec((1, width), lambda i: (0, 0))
    sums_spec = pl.BlockSpec((GROUP, HEAD), lambda i: (0, 0))
    table = pltpu.VMEM((heads, GROUP, GROUP), F32)
    state_shape = jax.ShapeDtypeStruct((devices, groups, HEAD // RING, HEAD), BF16)
    rows_shape = jax.ShapeDtypeStruct((rows, width), BF16)
    gain = gain.reshape(1, width)
    params = pltpu.CompilerParams(vmem_limit_bytes=40 << 20)

    def exchange(states, reverse, ident):
        dma = pltpu.SemaphoreType.DMA
        return pl.pallas_call(
            functools.partial(scan_kernel, RING, reverse),
            out_shape=state_shape,
            in_specs=[smem, smem, smem, pl.BlockSpec(memory_space=pl.ANY)],
            out_specs=pl.BlockSpec(memory_space=pl.ANY),
            scratch_shapes=[pltpu.VMEM((total_groups, HEAD // RING, HEAD), BF16)] * 3
            + [dma((devices - 1,))] * 4
            + [dma((2,))],
            compiler_params=pltpu.CompilerParams(
                collective_id=ident, has_side_effects=True, vmem_limit_bytes=40 << 20
            ),
        )(order, homes, carry, states)

    summaries = pl.pallas_call(
        functools.partial(summary_kernel, heads),
        grid=(groups,),
        out_shape=state_shape,
        in_specs=[smem, smem, seg_spec, row_spec, row_spec],
        out_specs=state_spec,
        scratch_shapes=[table],
        compiler_params=params,
    )(rate, edges, seg, k, v)
    prev = exchange(summaries, False, 0)
    out, sums = pl.pallas_call(
        functools.partial(output_kernel, heads),
        grid=(groups,),
        out_shape=(jax.ShapeDtypeStruct((rows, width), F32), jax.ShapeDtypeStruct((GROUP, HEAD), F32)),
        in_specs=[smem, smem, seg_spec, row_spec, row_spec, row_spec, row_spec, state_spec, gain_spec],
        out_specs=(row_spec, sums_spec),
        scratch_shapes=[table, table],
        compiler_params=params,
    )(rate, edges, seg, q, k, v, u, prev, gain)
    part = 2 * groups
    whole = pl.BlockSpec(memory_space=pltpu.VMEM)
    sums = pl.pallas_call(
        total_kernel,
        out_shape=jax.ShapeDtypeStruct((GROUP, HEAD), F32),
        in_specs=[whole],
        out_specs=whole,
        scratch_shapes=[
            pltpu.VMEM((part, HEAD), F32),
            pltpu.VMEM((sides - 1, part, HEAD), F32),
            pltpu.SemaphoreType.DMA((sides - 1,)),
            pltpu.SemaphoreType.DMA((sides - 1,)),
        ],
        compiler_params=pltpu.CompilerParams(collective_id=2, has_side_effects=True),
    )(sums)
    grad, rev = pl.pallas_call(
        functools.partial(cotangent_kernel, heads, width * sides),
        grid=(groups,),
        out_shape=(rows_shape, state_shape),
        in_specs=[smem, smem, seg_spec, row_spec, row_spec, row_spec, gain_spec, sums_spec],
        out_specs=(row_spec, state_spec),
        scratch_shapes=[table],
        compiler_params=params,
    )(rate, edges, seg, q, u, out, gain, sums)
    after = exchange(rev, True, 1)
    return pl.pallas_call(
        functools.partial(gradient_kernel, heads),
        grid=(groups,),
        out_shape=(rows_shape,) * 3,
        in_specs=[smem, smem, seg_spec, row_spec, row_spec, row_spec, row_spec, state_spec, state_spec],
        out_specs=(row_spec,) * 3,
        scratch_shapes=[table] * 3,
        compiler_params=params,
    )(rate, edges, seg, q, k, v, grad, prev, after)


def solution(mesh):
    rows = P("seq", "head")
    return jax.shard_map(
        shards,
        mesh=mesh,
        in_specs=(rows, rows, rows, rows, P("head"), P("head"), P(), P("seq")),
        out_specs=(rows, rows, rows),
        check_vma=False,
    )
```

```python
import functools

import jax
import jax.numpy as jnp
from jax import lax
from jax.experimental import pallas as pl
from jax.experimental.pallas import tpu as pltpu
from jax.sharding import PartitionSpec as P

HEAD = 128
GROUP = 128
RING = 4
CHUNK = 4
UNROLL = 8
EPSILON = 1e-06
MESH = pl.DeviceIdType.MESH
F32 = jnp.float32
BF16 = jnp.bfloat16
I32 = jnp.int32
NN = ((1,), (0,))
NT = ((1,), (1,))
TN = ((0,), (0,))


def dot(a, b, dims):
    return lax.dot_general(a, b, (dims, ((), ())), preferred_element_type=F32)


def cols_of(h):
    return slice(h * HEAD, (h + 1) * HEAD)


def iota(shape, dim):
    return lax.broadcasted_iota(I32, shape, dim)


def torus_offsets(ring):
    offsets = [(dy, dz) for dy in range(ring) for dz in range(ring) if (dy, dz) != (0, 0)]
    return sorted(offsets, key=lambda o: min(o[0], ring - o[0]) + min(o[1], ring - o[1]))


def wait_bytes(ref, sem):
    pltpu.make_async_copy(ref, ref, sem).wait()


def fused_kernel(
    heads, groups, devices, sides, docs,
    rate_ref, len_ref, home_ref, gain_ref, q_hbm, k_hbm, v_hbm, u_hbm,
    qo_hbm, ko_hbm, vo_hbm,
    q_ref, k_ref, v_ref, u_ref, send_ref, got1_ref, got2_ref, seq_ref, back_ref, prev_ref, after_ref,
    att_ref, vgp_ref, mix_ref, qout_ref, kout_ref, vout_ref,
    dec_ref, qdec_ref, kdec_ref, segr_ref, bef_ref, last_ref, segc_ref,
    hmine_ref, hall_ref, hcomp_ref, order_ref, carry_ref, homes_s, order_s, carry_s,
    mine_ref, gsum_ref,
    kv_sem, qu_sem, own_sem, smem_sem, hsend, hrecv, send1, recv1, send2, recv2,
    send3, recv3, send4, recv4, ssend, srecv, out_sem,
):
    me = lax.axis_index("seq")
    side = lax.axis_index("head")
    y, z = me // RING, lax.rem(me, RING)
    peers = [lax.rem(y + dy, RING) * RING + lax.rem(z + dz, RING) for dy, dz in torus_offsets(RING)]
    mates = [lax.rem(side + n, sides) for n in range(1, sides)]
    others = devices - 1
    total = devices * groups
    chunks = groups // CHUNK
    slab = CHUNK * GROUP
    part = HEAD // RING

    barrier = pltpu.get_barrier_semaphore()
    for peer in peers:
        pl.semaphore_signal(barrier, inc=1, device_id=(peer, side), device_id_type=MESH)
    for mate in mates:
        pl.semaphore_signal(barrier, inc=1, device_id=(me, mate), device_id_type=MESH)

    def slab_copy(hbm, ref, c, sem):
        rows = pl.ds(c * slab, slab)
        return pltpu.make_async_copy(hbm.at[rows], ref.at[rows], sem)

    for c in range(chunks):
        slab_copy(k_hbm, k_ref, c, kv_sem.at[0, c]).start()
        slab_copy(v_hbm, v_ref, c, kv_sem.at[1, c]).start()
    load_q = pltpu.make_async_copy(q_hbm, q_ref, qu_sem.at[0])
    load_u = pltpu.make_async_copy(u_hbm, u_ref, qu_sem.at[1])
    load_q.start()
    load_u.start()

    row = iota((GROUP, GROUP), 0).astype(F32)
    spread = row - iota((GROUP, GROUP), 1).astype(F32)
    for h in range(heads):
        r = rate_ref[h]
        dec_ref[h] = jnp.where(spread >= 0.0, jnp.exp(-r * jnp.maximum(spread, 0.0)), 0.0)
        qdec_ref[h] = jnp.exp(-r * (row + 1.0))
        kdec_ref[h] = jnp.exp(-r * (GROUP - 1.0 - row))

    home_rows = jnp.zeros((groups, HEAD), I32)
    home_lanes = jnp.zeros((8, HEAD), I32)
    group_row = iota((groups, HEAD), 0)
    lane8 = iota((8, HEAD), 1)
    for i in range(groups):
        home_rows = jnp.where(group_row == i, home_ref[i], home_rows)
        home_lanes = jnp.where(lane8 == i, home_ref[i], home_lanes)
    hmine_ref[...] = home_lanes
    hall_ref[me] = home_lanes
    steps = iota((8, HEAD), 0) * HEAD + lane8
    pos = home_rows * GROUP + iota((groups, HEAD), 1)
    pos_b = home_rows * GROUP - 1
    step_b = steps * GROUP - 1
    seg = jnp.zeros_like(pos)
    seg_b = jnp.zeros_like(pos)
    step_seg_b = jnp.zeros_like(steps)
    step_seg_e = jnp.zeros_like(steps)
    end = jnp.int32(0)
    for n in range(docs):
        end = end + len_ref[n]
        seg += (pos >= end).astype(I32)
        seg_b += (pos_b >= end).astype(I32)
        step_seg_b += (step_b >= end).astype(I32)
        step_seg_e += (step_b + GROUP >= end).astype(I32)
    seg_b = jnp.where(home_rows == 0, -1, seg_b).astype(F32)
    seg = seg.astype(F32)
    for i in range(groups):
        segr_ref[i] = seg[i : i + 1]
        bef_ref[i] = seg_b[i : i + 1]
        last_ref[i] = jnp.broadcast_to(seg[i : i + 1, GROUP - 1 :], (1, HEAD))
    own_rate = rate_ref[me // RING]
    keep = jnp.exp(jnp.zeros((8, HEAD), F32) - own_rate * GROUP)
    joined = (step_seg_b == step_seg_e) | (steps == 0)
    carry_ref[...] = jnp.where(joined, keep, 0.0)
    carry_copy = pltpu.make_async_copy(carry_ref, carry_s, smem_sem.at[0])
    carry_copy.start()

    pl.semaphore_wait(barrier, others + sides - 1)
    for peer in peers:
        pltpu.make_async_remote_copy(
            src_ref=hmine_ref, dst_ref=hall_ref.at[me], send_sem=hsend, recv_sem=hrecv,
            device_id=(peer, side), device_id_type=MESH,
        ).start()

    def rows_of(i):
        return pl.ds(pl.multiple_of(i * GROUP, GROUP), GROUP)

    def scatter_chunk(got_ref, c, send_sem, recv_sem):
        for peer in peers:
            pltpu.make_async_remote_copy(
                src_ref=send_ref.at[peer, pl.ds(c * CHUNK, CHUNK)],
                dst_ref=got_ref.at[pl.ds(me * groups + c * CHUNK, CHUNK)],
                send_sem=send_sem, recv_sem=recv_sem,
                device_id=(peer, side), device_id_type=MESH,
            ).start()

    def return_chunk(dst_ref, c, send_sem, recv_sem):
        for peer in peers:
            pltpu.make_async_remote_copy(
                src_ref=back_ref.at[pl.ds(peer * groups + c * CHUNK, CHUNK)],
                dst_ref=dst_ref.at[me, pl.ds(c * CHUNK, CHUNK)],
                send_sem=send_sem, recv_sem=recv_sem.at[c],
                device_id=(peer, side), device_id_type=MESH,
            ).start()

    def own_slice(got_ref, n):
        return pltpu.make_async_copy(send_ref.at[me], got_ref.at[pl.ds(me * groups, groups)], own_sem.at[n])

    def own_back(dst_ref, n):
        return pltpu.make_async_copy(back_ref.at[pl.ds(me * groups, groups)], dst_ref.at[me], own_sem.at[n])

    def store_state(i, h, s):
        send_ref[RING * h : RING * (h + 1), i] = s.astype(BF16).reshape(RING, part, HEAD)

    def state_of(ref, i, h):
        return ref[RING * h : RING * (h + 1), i].reshape(HEAD, HEAD)

    def summary_group(i, _):
        rows = rows_of(i)
        seg_c = jnp.broadcast_to(segr_ref[i], (GROUP, GROUP)).T
        segc_ref[i] = seg_c
        live = seg_c == last_ref[i]
        for h in range(heads):
            cols = cols_of(h)
            w = (jnp.where(live, kdec_ref[h], 0.0) * v_ref[rows, cols].astype(F32)).astype(BF16)
            store_state(i, h, dot(k_ref[rows, cols], w, TN))
        return 0

    def summary_chunk(c, _):
        slab_copy(k_hbm, k_ref, c, kv_sem.at[0, c]).wait()
        slab_copy(v_hbm, v_ref, c, kv_sem.at[1, c]).wait()
        lax.fori_loop(c * CHUNK, (c + 1) * CHUNK, summary_group, 0)
        scatter_chunk(got1_ref, c, send1, recv1)
        return 0

    lax.fori_loop(0, chunks, summary_chunk, 0)
    own_slice(got1_ref, 0).start()

    wait_bytes(hall_ref.at[pl.ds(0, others)], hrecv)
    for d in range(devices):
        hcomp_ref[d : d + 1] = hall_ref[d, 0:1]
    homes_copy = pltpu.make_async_copy(hcomp_ref, homes_s, smem_sem.at[1])
    homes_copy.start()
    homes_copy.wait()

    def invert(b, acc):
        for n in range(UNROLL):
            p = b * UNROLL + n
            acc = jnp.where(steps == homes_s[p // groups, lax.rem(p, groups)], p, acc)
        return acc

    order_ref[...] = lax.fori_loop(0, total // UNROLL, invert, jnp.zeros((8, HEAD), I32))
    order_copy = pltpu.make_async_copy(order_ref, order_s, smem_sem.at[2])
    order_copy.start()
    load_q.wait()
    load_u.wait()

    def inner_group(i, _):
        rows = rows_of(i)
        same = segc_ref[i] == segr_ref[i]
        for h in range(heads):
            cols = cols_of(h)
            scores = dot(q_ref[rows, cols], k_ref[rows, cols], NT)
            mixing = (scores * jnp.where(same, dec_ref[h], 0.0)).astype(BF16)
            mix_ref[i * heads + h] = mixing
            att_ref[rows, cols] = dot(mixing, v_ref[rows, cols], NN)
        return 0

    lax.fori_loop(0, groups, inner_group, 0)
    order_copy.wait()
    carry_copy.wait()

    def scan(got_ref, reverse):
        def step(b, state):
            b = total // UNROLL - 1 - b if reverse else b
            for n in range(UNROLL):
                t = b * UNROLL + (UNROLL - 1 - n if reverse else n)
                hi, lo = t // HEAD, lax.rem(t, HEAD)
                seq_ref[t] = state.astype(BF16)
                state = carry_s[hi, lo] * state + got_ref[order_s[hi, lo]].astype(F32)
            return state

        lax.fori_loop(0, total // UNROLL, step, jnp.zeros((part, HEAD), F32))

        def put(b, _):
            for n in range(UNROLL):
                p = b * UNROLL + n
                back_ref[p] = seq_ref[homes_s[p // groups, lax.rem(p, groups)]]
            return 0

        lax.fori_loop(0, total // UNROLL, put, 0)

    own_slice(got1_ref, 0).wait()
    wait_bytes(got1_ref.at[pl.ds(0, others * groups)], recv1)
    scan(got1_ref, False)

    def return_all(dst_ref, send_sem, recv_sem):
        def body(c, _):
            return_chunk(dst_ref, c, send_sem, recv_sem)
            return 0

        lax.fori_loop(0, chunks, body, 0)

    return_all(prev_ref, send2, recv2)
    own_back(prev_ref, 1).start()
    wait_bytes(send_ref.at[pl.ds(0, others)], send1)
    wait_bytes(hall_ref.at[pl.ds(0, others)], hsend)
    own_back(prev_ref, 1).wait()

    lane = iota((GROUP, HEAD), 1)
    pieces = GROUP // (2 * CHUNK)
    width = 2 * CHUNK

    def output_group(c, g, acc):
        i = c * CHUNK + g
        rows = rows_of(i)
        live = segc_ref[i] == bef_ref[i]
        squares = jnp.zeros((GROUP, HEAD), F32)
        crossed = jnp.zeros((GROUP, HEAD), F32)
        for h in range(heads):
            cols = cols_of(h)
            carried = dot(q_ref[rows, cols], state_of(prev_ref, i, h), NN)
            out = att_ref[rows, cols] + jnp.where(live, qdec_ref[h], 0.0) * carried
            att_ref[rows, cols] = out
            squares += out * out
            crossed += gain_ref[:, cols] * u_ref[rows, cols].astype(F32) * out
        squares = jnp.sum(squares, axis=1, keepdims=True)
        crossed = jnp.sum(crossed, axis=1, keepdims=True)
        return jnp.where(lane == g, squares, jnp.where(lane == g + CHUNK, crossed, acc))

    def total_copy(c, n):
        return pltpu.make_async_remote_copy(
            src_ref=mine_ref.at[c], dst_ref=gsum_ref.at[c, n], send_sem=ssend.at[c], recv_sem=srecv.at[c],
            device_id=(me, mates[n]), device_id_type=MESH,
        )

    def output_chunk(c):
        wait_bytes(prev_ref.at[pl.ds(0, others), pl.ds(c * CHUNK, CHUNK)], recv2.at[c])
        acc = lax.fori_loop(0, CHUNK, functools.partial(output_group, c), jnp.zeros((GROUP, HEAD), F32))
        packed = acc[0:width]
        for n in range(1, pieces):
            packed += pltpu.roll(acc[n * width : (n + 1) * width], n * width, 1)
        mine_ref[c] = packed
        for n in range(sides - 1):
            total_copy(c, n).start()

    channels = heads * HEAD * sides

    def cotangent_group(c, sums, g, _):
        i = c * CHUNK + g
        rows = rows_of(i)
        live = segc_ref[i] == bef_ref[i]
        squares = jnp.sum(jnp.where(lane == g, sums, 0.0), axis=1, keepdims=True)
        crossed = jnp.sum(jnp.where(lane == g + CHUNK, sums, 0.0), axis=1, keepdims=True)
        scaling = lax.rsqrt(squares / channels + EPSILON)
        pull = scaling * scaling * scaling * (crossed / channels)
        for h in range(heads):
            cols = cols_of(h)
            wide = gain_ref[:, cols] * u_ref[rows, cols].astype(F32)
            grad = (scaling * wide - pull * att_ref[rows, cols]).astype(BF16)
            u_ref[rows, cols] = grad
            w = (jnp.where(live, qdec_ref[h], 0.0) * grad.astype(F32)).astype(BF16)
            store_state(i, h, dot(q_ref[rows, cols], w, TN))
        return 0

    def cotangent_chunk(c):
        wait_bytes(gsum_ref.at[c], srecv.at[c])
        wait_bytes(gsum_ref.at[c], ssend.at[c])
        both = mine_ref[c]
        for n in range(sides - 1):
            both += gsum_ref[c, n]
        sums = jnp.concatenate(
            [both] + [pltpu.roll(both, HEAD - n * width, 1) for n in range(1, pieces)], axis=0
        )
        lax.fori_loop(0, CHUNK, functools.partial(cotangent_group, c, sums), 0)
        scatter_chunk(got2_ref, c, send3, recv3)

    def middle(c, _):
        @pl.when(c < chunks)
        def _():
            output_chunk(c)

        @pl.when(c >= 1)
        def _():
            cotangent_chunk(c - 1)

        return 0

    lax.fori_loop(0, chunks + 1, middle, 0)
    own_slice(got2_ref, 2).start()

    def local_group(i, _):
        rows = rows_of(i)
        seg_c = segc_ref[i]
        same = seg_c == segr_ref[i]
        live = seg_c == bef_ref[i]
        for h in range(heads):
            cols = cols_of(h)
            g, k, q = u_ref[rows, cols], k_ref[rows, cols], q_ref[rows, cols]
            score = (dot(g, v_ref[rows, cols], NT) * jnp.where(same, dec_ref[h], 0.0)).astype(BF16)
            carried = jnp.where(live, qdec_ref[h], 0.0) * dot(g, state_of(prev_ref, i, h), NT)
            qout_ref[rows, cols] = (dot(score, k, NN) + carried).astype(BF16)
            att_ref[rows, cols] = dot(score, q, TN)
            vgp_ref[rows, cols] = dot(mix_ref[i * heads + h], g, TN)
        return 0

    early = groups // 2
    lax.fori_loop(0, early, local_group, 0)
    for c in range(chunks):
        wait_bytes(prev_ref.at[pl.ds(0, others), pl.ds(0, CHUNK)], send2)
    own_slice(got2_ref, 2).wait()
    wait_bytes(got2_ref.at[pl.ds(0, others * groups)], recv3)
    scan(got2_ref, True)
    return_all(after_ref, send4, recv4)
    own_back(after_ref, 3).start()
    lax.fori_loop(early, groups, local_group, 0)
    store_q = pltpu.make_async_copy(qout_ref, qo_hbm, out_sem.at[2, 0])
    store_q.start()
    own_back(after_ref, 3).wait()

    def final_group(i, _):
        rows = rows_of(i)
        live = segc_ref[i] == last_ref[i]
        for h in range(heads):
            cols = cols_of(h)
            after = state_of(after_ref, i, h)
            w = jnp.where(live, kdec_ref[h], 0.0)
            kout_ref[rows, cols] = (att_ref[rows, cols] + w * dot(v_ref[rows, cols], after, NT)).astype(BF16)
            vout_ref[rows, cols] = (vgp_ref[rows, cols] + w * dot(k_ref[rows, cols], after, NN)).astype(BF16)
        return 0

    def final_chunk(c, _):
        wait_bytes(after_ref.at[pl.ds(0, others), pl.ds(c * CHUNK, CHUNK)], recv4.at[c])
        lax.fori_loop(c * CHUNK, (c + 1) * CHUNK, final_group, 0)
        rows = pl.ds(c * slab, slab)
        pltpu.make_async_copy(kout_ref.at[rows], ko_hbm.at[rows], out_sem.at[0, c]).start()
        pltpu.make_async_copy(vout_ref.at[rows], vo_hbm.at[rows], out_sem.at[1, c]).start()
        return 0

    lax.fori_loop(0, chunks, final_chunk, 0)
    store_q.wait()
    for c in range(chunks):
        rows = pl.ds(c * slab, slab)
        pltpu.make_async_copy(kout_ref.at[rows], ko_hbm.at[rows], out_sem.at[0, c]).wait()
        pltpu.make_async_copy(vout_ref.at[rows], vo_hbm.at[rows], out_sem.at[1, c]).wait()
    wait_bytes(send_ref.at[pl.ds(0, others)], send3)
    wait_bytes(send_ref.at[pl.ds(0, others)], send4)


def shards(q, k, v, u, gain, rate, lengths, home):
    devices = lax.axis_size("seq")
    sides = lax.axis_size("head")
    heads = q.shape[1] // HEAD
    groups = home.shape[0]
    rows, width = q.shape
    docs = lengths.shape[0]
    total = devices * groups
    chunks = groups // CHUNK
    part = HEAD // RING
    smem = pl.BlockSpec(memory_space=pltpu.SMEM)
    any_ = pl.BlockSpec(memory_space=pl.ANY)
    vmem, dma = pltpu.VMEM, pltpu.SemaphoreType.DMA
    table = vmem((heads, GROUP, GROUP), F32)
    strip = vmem((groups, 1, HEAD), F32)
    token = vmem((rows, width), BF16)
    flat = vmem((total, part, HEAD), BF16)
    state = vmem((devices, groups, part, HEAD), BF16)
    wide = vmem((rows, width), F32)
    scratch = (
        [token] * 4 + [state, flat, flat, flat, flat, state, state]
        + [wide, wide, vmem((groups * heads, GROUP, GROUP), BF16)] + [token] * 3
        + [table] * 3 + [strip] * 3 + [vmem((groups, GROUP, GROUP), F32)]
        + [vmem((8, HEAD), I32), vmem((devices, 8, HEAD), I32), vmem((devices, HEAD), I32)]
        + [vmem((8, HEAD), I32), vmem((8, HEAD), F32)]
        + [pltpu.SMEM((devices, HEAD), I32), pltpu.SMEM((8, HEAD), I32), pltpu.SMEM((8, HEAD), F32)]
        + [vmem((chunks, 2 * CHUNK, HEAD), F32), vmem((chunks, sides - 1, 2 * CHUNK, HEAD), F32)]
        + [dma((2, chunks)), dma((2,)), dma((4,)), dma((3,)), dma, dma, dma, dma, dma, dma((chunks,))]
        + [dma, dma, dma, dma((chunks,)), dma((chunks,)), dma((chunks,)), dma((3, chunks))]
    )
    return pl.pallas_call(
        functools.partial(fused_kernel, heads, groups, devices, sides, docs),
        out_shape=(jax.ShapeDtypeStruct((rows, width), BF16),) * 3,
        in_specs=[smem, smem, smem, pl.BlockSpec(memory_space=vmem)] + [any_] * 4,
        out_specs=(any_,) * 3,
        scratch_shapes=scratch,
        compiler_params=pltpu.CompilerParams(
            collective_id=0, has_side_effects=True, vmem_limit_bytes=52 << 20
        ),
    )(rate, lengths, home, gain.reshape(1, width), q, k, v, u)


def solution(mesh):
    rows = P("seq", "head")
    return jax.shard_map(
        shards,
        mesh=mesh,
        in_specs=(rows, rows, rows, rows, P("head"), P("head"), P(), P("seq")),
        out_specs=(rows, rows, rows),
        check_vma=False,
    )
```

```python
import functools

import jax
import jax.numpy as jnp
from jax import lax
from jax.experimental import pallas as pl
from jax.experimental.pallas import tpu as pltpu
from jax.sharding import PartitionSpec as P

HEAD = 128
GROUP = 128
RING = 4
CHUNK = 4
UNROLL = 8
EPSILON = 1e-06
MESH = pl.DeviceIdType.MESH
F32 = jnp.float32
BF16 = jnp.bfloat16
I32 = jnp.int32
NN = ((1,), (0,))
NT = ((1,), (1,))
TN = ((0,), (0,))


def dot(a, b, dims):
    return lax.dot_general(a, b, (dims, ((), ())), preferred_element_type=F32)


def cols_of(h):
    return slice(h * HEAD, (h + 1) * HEAD)


def iota(shape, dim):
    return lax.broadcasted_iota(I32, shape, dim)


def torus_offsets(ring):
    offsets = [(dy, dz) for dy in range(ring) for dz in range(ring) if (dy, dz) != (0, 0)]
    return sorted(offsets, key=lambda o: min(o[0], ring - o[0]) + min(o[1], ring - o[1]))


def wait_bytes(ref, sem):
    pltpu.make_async_copy(ref, ref, sem).wait()


def fused_kernel(
    heads, groups, devices, sides, docs,
    rate_ref, len_ref, home_ref, gain_ref, q_hbm, k_hbm, v_hbm, u_hbm,
    qo_hbm, ko_hbm, vo_hbm,
    q_ref, k_ref, v_ref, u_ref, send_ref, got1a_ref, got1b_ref, got2a_ref, got2b_ref, seq_ref, back_ref, prev_ref, after_ref,
    att_ref, vgp_ref, mix_ref, qout_ref, kout_ref, vout_ref,
    dec_ref, qdec_ref, kdec_ref, segr_ref, bef_ref, last_ref, segc_ref,
    hmine_ref, hall_ref, hcomp_ref, order_ref, carry_ref, homes_s, order_s, carry_s,
    mine_ref, gsum_ref,
    kv_sem, qu_sem, own_sem, smem_sem, hsend, hrecv, send1, recv1, send2, recv2a, recv2b,
    send3, recv3, send4, recv4a, recv4b, ssend, srecv, out_sem,
):
    me = lax.axis_index("seq")
    side = lax.axis_index("head")
    y, z = me // RING, lax.rem(me, RING)
    peers = [lax.rem(y + dy, RING) * RING + lax.rem(z + dz, RING) for dy, dz in torus_offsets(RING)]
    mates = [lax.rem(side + n, sides) for n in range(1, sides)]
    got1_ref, got2_ref = (got1a_ref, got1b_ref), (got2a_ref, got2b_ref)
    others = devices - 1
    total = devices * groups
    chunks = groups // CHUNK
    slab = CHUNK * GROUP
    part = HEAD // RING // 2

    barrier = pltpu.get_barrier_semaphore()
    for peer in peers:
        pl.semaphore_signal(barrier, inc=1, device_id=(peer, side), device_id_type=MESH)
    for mate in mates:
        pl.semaphore_signal(barrier, inc=1, device_id=(me, mate), device_id_type=MESH)

    def slab_copy(hbm, ref, c, sem):
        rows = pl.ds(c * slab, slab)
        return pltpu.make_async_copy(hbm.at[rows], ref.at[rows], sem)

    for c in range(chunks):
        slab_copy(k_hbm, k_ref, c, kv_sem.at[0, c]).start()
        slab_copy(v_hbm, v_ref, c, kv_sem.at[1, c]).start()
    load_q = pltpu.make_async_copy(q_hbm, q_ref, qu_sem.at[0])
    load_u = pltpu.make_async_copy(u_hbm, u_ref, qu_sem.at[1])
    load_q.start()
    load_u.start()

    row = iota((GROUP, GROUP), 0).astype(F32)
    spread = row - iota((GROUP, GROUP), 1).astype(F32)
    for h in range(heads):
        r = rate_ref[h]
        dec_ref[h] = jnp.where(spread >= 0.0, jnp.exp(-r * jnp.maximum(spread, 0.0)), 0.0)
        qdec_ref[h] = jnp.exp(-r * (row + 1.0))
        kdec_ref[h] = jnp.exp(-r * (GROUP - 1.0 - row))

    home_rows = jnp.zeros((groups, HEAD), I32)
    home_lanes = jnp.zeros((8, HEAD), I32)
    group_row = iota((groups, HEAD), 0)
    lane8 = iota((8, HEAD), 1)
    for i in range(groups):
        home_rows = jnp.where(group_row == i, home_ref[i], home_rows)
        home_lanes = jnp.where(lane8 == i, home_ref[i], home_lanes)
    hmine_ref[...] = home_lanes
    hall_ref[me] = home_lanes
    steps = iota((8, HEAD), 0) * HEAD + lane8
    pos = home_rows * GROUP + iota((groups, HEAD), 1)
    pos_b = home_rows * GROUP - 1
    step_b = steps * GROUP - 1
    seg = jnp.zeros_like(pos)
    seg_b = jnp.zeros_like(pos)
    step_seg_b = jnp.zeros_like(steps)
    step_seg_e = jnp.zeros_like(steps)
    end = jnp.int32(0)
    for n in range(docs):
        end = end + len_ref[n]
        seg += (pos >= end).astype(I32)
        seg_b += (pos_b >= end).astype(I32)
        step_seg_b += (step_b >= end).astype(I32)
        step_seg_e += (step_b + GROUP >= end).astype(I32)
    seg_b = jnp.where(home_rows == 0, -1, seg_b).astype(F32)
    seg = seg.astype(F32)
    for i in range(groups):
        segr_ref[i] = seg[i : i + 1]
        bef_ref[i] = seg_b[i : i + 1]
        last_ref[i] = jnp.broadcast_to(seg[i : i + 1, GROUP - 1 :], (1, HEAD))
    own_rate = rate_ref[me // RING]
    keep = jnp.exp(jnp.zeros((8, HEAD), F32) - own_rate * GROUP)
    joined = (step_seg_b == step_seg_e) | (steps == 0)
    carry_ref[...] = jnp.where(joined, keep, 0.0)
    carry_copy = pltpu.make_async_copy(carry_ref, carry_s, smem_sem.at[0])
    carry_copy.start()

    pl.semaphore_wait(barrier, others + sides - 1)
    for peer in peers:
        pltpu.make_async_remote_copy(
            src_ref=hmine_ref, dst_ref=hall_ref.at[me], send_sem=hsend, recv_sem=hrecv,
            device_id=(peer, side), device_id_type=MESH,
        ).start()

    def rows_of(i):
        return pl.ds(pl.multiple_of(i * GROUP, GROUP), GROUP)

    def scatter(got_ref, half, c, send_sem, recv_sem):
        for peer in peers:
            pltpu.make_async_remote_copy(
                src_ref=send_ref.at[half, peer, pl.ds(c * CHUNK, CHUNK)],
                dst_ref=got_ref[half].at[pl.ds(me * groups + c * CHUNK, CHUNK)],
                send_sem=send_sem, recv_sem=recv_sem.at[half],
                device_id=(peer, side), device_id_type=MESH,
            ).start()

    def give_back(dst_ref, half, start, size, send_sem, recv_sem):
        for peer in peers:
            pltpu.make_async_remote_copy(
                src_ref=back_ref.at[half, pl.ds(peer * groups + start, size)],
                dst_ref=dst_ref.at[half, me, pl.ds(start, size)],
                send_sem=send_sem, recv_sem=recv_sem,
                device_id=(peer, side), device_id_type=MESH,
            ).start()

    def own_slice(got_ref, half, n):
        return pltpu.make_async_copy(
            send_ref.at[half, me], got_ref[half].at[pl.ds(me * groups, groups)], own_sem.at[n, half]
        )

    def own_back(dst_ref, half, n):
        return pltpu.make_async_copy(
            back_ref.at[half, pl.ds(me * groups, groups)], dst_ref.at[half, me], own_sem.at[n, half]
        )

    def store_state(i, h, s):
        send_ref[:, RING * h : RING * (h + 1), i] = s.astype(BF16).reshape(2, RING, part, HEAD)

    def state_of(ref, i, h):
        return ref[:, RING * h : RING * (h + 1), i].reshape(HEAD, HEAD)

    def summary_group(i, _):
        rows = rows_of(i)
        seg_c = jnp.broadcast_to(segr_ref[i], (GROUP, GROUP)).T
        segc_ref[i] = seg_c
        live = seg_c == last_ref[i]
        for h in range(heads):
            cols = cols_of(h)
            w = (jnp.where(live, kdec_ref[h], 0.0) * v_ref[rows, cols].astype(F32)).astype(BF16)
            store_state(i, h, dot(k_ref[rows, cols], w, TN))
        return 0

    def summary_chunk(c, _):
        slab_copy(k_hbm, k_ref, c, kv_sem.at[0, c]).wait()
        slab_copy(v_hbm, v_ref, c, kv_sem.at[1, c]).wait()
        lax.fori_loop(c * CHUNK, (c + 1) * CHUNK, summary_group, 0)
        scatter(got1_ref, 0, c, send1, recv1)
        return 0

    lax.fori_loop(0, chunks, summary_chunk, 0)

    def second_half(c, _):
        scatter(got1_ref, 1, c, send1, recv1)
        return 0

    lax.fori_loop(0, chunks, second_half, 0)
    own_slice(got1_ref, 0, 0).start()
    own_slice(got1_ref, 1, 0).start()

    wait_bytes(hall_ref.at[pl.ds(0, others)], hrecv)
    for d in range(devices):
        hcomp_ref[d : d + 1] = hall_ref[d, 0:1]
    homes_copy = pltpu.make_async_copy(hcomp_ref, homes_s, smem_sem.at[1])
    homes_copy.start()
    homes_copy.wait()

    def invert(b, acc):
        for n in range(UNROLL):
            p = b * UNROLL + n
            acc = jnp.where(steps == homes_s[p // groups, lax.rem(p, groups)], p, acc)
        return acc

    order_ref[...] = lax.fori_loop(0, total // UNROLL, invert, jnp.zeros((8, HEAD), I32))
    order_copy = pltpu.make_async_copy(order_ref, order_s, smem_sem.at[2])
    order_copy.start()
    load_q.wait()
    load_u.wait()

    def inner_group(i, _):
        rows = rows_of(i)
        same = segc_ref[i] == segr_ref[i]
        for h in range(heads):
            cols = cols_of(h)
            scores = dot(q_ref[rows, cols], k_ref[rows, cols], NT)
            mixing = (scores * jnp.where(same, dec_ref[h], 0.0)).astype(BF16)
            mix_ref[i * heads + h] = mixing
            att_ref[rows, cols] = dot(mixing, v_ref[rows, cols], NN)
        return 0

    lax.fori_loop(0, groups, inner_group, 0)
    order_copy.wait()
    carry_copy.wait()

    def scan(got_ref, half, reverse):
        def step(b, state):
            b = total // UNROLL - 1 - b if reverse else b
            for n in range(UNROLL):
                t = b * UNROLL + (UNROLL - 1 - n if reverse else n)
                hi, lo = t // HEAD, lax.rem(t, HEAD)
                seq_ref[t] = state.astype(BF16)
                state = carry_s[hi, lo] * state + got_ref[half][order_s[hi, lo]].astype(F32)
            return state

        lax.fori_loop(0, total // UNROLL, step, jnp.zeros((part, HEAD), F32))

        def put(b, _):
            for n in range(UNROLL):
                p = b * UNROLL + n
                back_ref[half, p] = seq_ref[homes_s[p // groups, lax.rem(p, groups)]]
            return 0

        lax.fori_loop(0, total // UNROLL, put, 0)

    half_groups = groups // 2

    def turn(got_ref, dst_ref, n, reverse, recv_sem, send_back, recv_first, recv_second):
        own_slice(got_ref, 0, n).wait()
        wait_bytes(got_ref[0].at[pl.ds(0, others * groups)], recv_sem.at[0])
        scan(got_ref, 0, reverse)
        give_back(dst_ref, 0, 0, half_groups, send_back, recv_first.at[0])
        own_back(dst_ref, 0, n + 1).start()
        own_slice(got_ref, 1, n).wait()
        wait_bytes(got_ref[1].at[pl.ds(0, others * groups)], recv_sem.at[1])
        scan(got_ref, 1, reverse)
        own_back(dst_ref, 1, n + 1).start()

        def rest(c, _):
            @pl.when(c == chunks // 2)
            def _():
                give_back(dst_ref, 0, half_groups, half_groups, send_back, recv_first.at[1])

            give_back(dst_ref, 1, c * CHUNK, CHUNK, send_back, recv_second.at[c])
            return 0

        lax.fori_loop(0, chunks, rest, 0)

    def turned(dst_ref, c, recv_first, recv_second):
        @pl.when(lax.rem(c, chunks // 2) == 0)
        def _():
            wait_bytes(
                dst_ref.at[0, pl.ds(0, others), pl.ds(0, half_groups)], recv_first.at[c // (chunks // 2)]
            )

        wait_bytes(dst_ref.at[1, pl.ds(0, others), pl.ds(0, CHUNK)], recv_second.at[c])

    def sent(sem):
        wait_bytes(send_ref.at[0, pl.ds(0, others)], sem)
        wait_bytes(send_ref.at[0, pl.ds(0, others)], sem)

    turn(got1_ref, prev_ref, 0, False, recv1, send2, recv2a, recv2b)
    sent(send1)
    wait_bytes(hall_ref.at[pl.ds(0, others)], hsend)
    own_back(prev_ref, 0, 1).wait()
    own_back(prev_ref, 1, 1).wait()

    lane = iota((GROUP, HEAD), 1)
    pieces = GROUP // (2 * CHUNK)
    width = 2 * CHUNK

    def output_group(c, g, acc):
        i = c * CHUNK + g
        rows = rows_of(i)
        live = segc_ref[i] == bef_ref[i]
        squares = jnp.zeros((GROUP, HEAD), F32)
        crossed = jnp.zeros((GROUP, HEAD), F32)
        for h in range(heads):
            cols = cols_of(h)
            carried = dot(q_ref[rows, cols], state_of(prev_ref, i, h), NN)
            out = att_ref[rows, cols] + jnp.where(live, qdec_ref[h], 0.0) * carried
            att_ref[rows, cols] = out
            squares += out * out
            crossed += gain_ref[:, cols] * u_ref[rows, cols].astype(F32) * out
        squares = jnp.sum(squares, axis=1, keepdims=True)
        crossed = jnp.sum(crossed, axis=1, keepdims=True)
        return jnp.where(lane == g, squares, jnp.where(lane == g + CHUNK, crossed, acc))

    def total_copy(c, n):
        return pltpu.make_async_remote_copy(
            src_ref=mine_ref.at[c], dst_ref=gsum_ref.at[c, n], send_sem=ssend.at[c], recv_sem=srecv.at[c],
            device_id=(me, mates[n]), device_id_type=MESH,
        )

    def output_chunk(c):
        turned(prev_ref, c, recv2a, recv2b)
        acc = lax.fori_loop(0, CHUNK, functools.partial(output_group, c), jnp.zeros((GROUP, HEAD), F32))
        packed = acc[0:width]
        for n in range(1, pieces):
            packed += pltpu.roll(acc[n * width : (n + 1) * width], n * width, 1)
        mine_ref[c] = packed
        for n in range(sides - 1):
            total_copy(c, n).start()

    channels = heads * HEAD * sides

    def cotangent_group(c, sums, g, _):
        i = c * CHUNK + g
        rows = rows_of(i)
        live = segc_ref[i] == bef_ref[i]
        squares = jnp.sum(jnp.where(lane == g, sums, 0.0), axis=1, keepdims=True)
        crossed = jnp.sum(jnp.where(lane == g + CHUNK, sums, 0.0), axis=1, keepdims=True)
        scaling = lax.rsqrt(squares / channels + EPSILON)
        pull = scaling * scaling * scaling * (crossed / channels)
        for h in range(heads):
            cols = cols_of(h)
            wide = gain_ref[:, cols] * u_ref[rows, cols].astype(F32)
            grad = (scaling * wide - pull * att_ref[rows, cols]).astype(BF16)
            u_ref[rows, cols] = grad
            w = (jnp.where(live, qdec_ref[h], 0.0) * grad.astype(F32)).astype(BF16)
            store_state(i, h, dot(q_ref[rows, cols], w, TN))
        return 0

    def cotangent_chunk(c):
        wait_bytes(gsum_ref.at[c], srecv.at[c])
        wait_bytes(gsum_ref.at[c], ssend.at[c])
        both = mine_ref[c]
        for n in range(sides - 1):
            both += gsum_ref[c, n]
        sums = jnp.concatenate(
            [both] + [pltpu.roll(both, HEAD - n * width, 1) for n in range(1, pieces)], axis=0
        )
        lax.fori_loop(0, CHUNK, functools.partial(cotangent_group, c, sums), 0)
        scatter(got2_ref, 0, c, send3, recv3)

        @pl.when(c < chunks - 2)
        def _():
            scatter(got2_ref, 1, c, send3, recv3)

    def middle(c, _):
        @pl.when(c < chunks)
        def _():
            output_chunk(c)

        @pl.when(c >= 1)
        def _():
            cotangent_chunk(c - 1)

        return 0

    lax.fori_loop(0, chunks + 1, middle, 0)
    for c in (chunks - 2, chunks - 1):
        scatter(got2_ref, 1, c, send3, recv3)
    own_slice(got2_ref, 0, 2).start()
    own_slice(got2_ref, 1, 2).start()

    def local_group(i, _):
        rows = rows_of(i)
        seg_c = segc_ref[i]
        same = seg_c == segr_ref[i]
        live = seg_c == bef_ref[i]
        for h in range(heads):
            cols = cols_of(h)
            g, k, q = u_ref[rows, cols], k_ref[rows, cols], q_ref[rows, cols]
            score = (dot(g, v_ref[rows, cols], NT) * jnp.where(same, dec_ref[h], 0.0)).astype(BF16)
            carried = jnp.where(live, qdec_ref[h], 0.0) * dot(g, state_of(prev_ref, i, h), NT)
            qout_ref[rows, cols] = (dot(score, k, NN) + carried).astype(BF16)
            att_ref[rows, cols] = dot(score, q, TN)
            vgp_ref[rows, cols] = dot(mix_ref[i * heads + h], g, TN)
        return 0

    early = groups // 2
    lax.fori_loop(0, early, local_group, 0)
    sent(send2)
    turn(got2_ref, after_ref, 2, True, recv3, send4, recv4a, recv4b)
    lax.fori_loop(early, groups, local_group, 0)
    store_q = pltpu.make_async_copy(qout_ref, qo_hbm, out_sem.at[2, 0])
    store_q.start()
    own_back(after_ref, 0, 3).wait()
    own_back(after_ref, 1, 3).wait()

    def final_group(i, _):
        rows = rows_of(i)
        live = segc_ref[i] == last_ref[i]
        for h in range(heads):
            cols = cols_of(h)
            after = state_of(after_ref, i, h)
            w = jnp.where(live, kdec_ref[h], 0.0)
            kout_ref[rows, cols] = (att_ref[rows, cols] + w * dot(v_ref[rows, cols], after, NT)).astype(BF16)
            vout_ref[rows, cols] = (vgp_ref[rows, cols] + w * dot(k_ref[rows, cols], after, NN)).astype(BF16)
        return 0

    def final_chunk(c, _):
        turned(after_ref, c, recv4a, recv4b)
        lax.fori_loop(c * CHUNK, (c + 1) * CHUNK, final_group, 0)
        rows = pl.ds(c * slab, slab)
        pltpu.make_async_copy(kout_ref.at[rows], ko_hbm.at[rows], out_sem.at[0, c]).start()
        pltpu.make_async_copy(vout_ref.at[rows], vo_hbm.at[rows], out_sem.at[1, c]).start()
        return 0

    lax.fori_loop(0, chunks, final_chunk, 0)
    store_q.wait()
    for c in range(chunks):
        rows = pl.ds(c * slab, slab)
        pltpu.make_async_copy(kout_ref.at[rows], ko_hbm.at[rows], out_sem.at[0, c]).wait()
        pltpu.make_async_copy(vout_ref.at[rows], vo_hbm.at[rows], out_sem.at[1, c]).wait()
    sent(send3)
    sent(send4)


def shards(q, k, v, u, gain, rate, lengths, home):
    devices = lax.axis_size("seq")
    sides = lax.axis_size("head")
    heads = q.shape[1] // HEAD
    groups = home.shape[0]
    rows, width = q.shape
    docs = lengths.shape[0]
    total = devices * groups
    chunks = groups // CHUNK
    part = HEAD // RING // 2
    smem = pl.BlockSpec(memory_space=pltpu.SMEM)
    any_ = pl.BlockSpec(memory_space=pl.ANY)
    vmem, dma = pltpu.VMEM, pltpu.SemaphoreType.DMA
    table = vmem((heads, GROUP, GROUP), F32)
    strip = vmem((groups, 1, HEAD), F32)
    token = vmem((rows, width), BF16)
    flat = vmem((total, part, HEAD), BF16)
    state = vmem((2, devices, groups, part, HEAD), BF16)
    wide = vmem((rows, width), F32)
    scratch = (
        [token] * 4 + [state] + [flat] * 5 + [vmem((2, total, part, HEAD), BF16), state, state]
        + [wide, wide, vmem((groups * heads, GROUP, GROUP), BF16)] + [token] * 3
        + [table] * 3 + [strip] * 3 + [vmem((groups, GROUP, GROUP), F32)]
        + [vmem((8, HEAD), I32), vmem((devices, 8, HEAD), I32), vmem((devices, HEAD), I32)]
        + [vmem((8, HEAD), I32), vmem((8, HEAD), F32)]
        + [pltpu.SMEM((devices, HEAD), I32), pltpu.SMEM((8, HEAD), I32), pltpu.SMEM((8, HEAD), F32)]
        + [vmem((chunks, 2 * CHUNK, HEAD), F32), vmem((chunks, sides - 1, 2 * CHUNK, HEAD), F32)]
        + [dma((2, chunks)), dma((2,)), dma((4, 2)), dma((3,)), dma, dma]
        + [dma, dma((2,)), dma, dma((2,)), dma((chunks,))] * 2
        + [dma((chunks,)), dma((chunks,)), dma((3, chunks))]
    )
    return pl.pallas_call(
        functools.partial(fused_kernel, heads, groups, devices, sides, docs),
        out_shape=(jax.ShapeDtypeStruct((rows, width), BF16),) * 3,
        in_specs=[smem, smem, smem, pl.BlockSpec(memory_space=vmem)] + [any_] * 4,
        out_specs=(any_,) * 3,
        scratch_shapes=scratch,
        compiler_params=pltpu.CompilerParams(
            collective_id=0, has_side_effects=True, vmem_limit_bytes=52 << 20
        ),
    )(rate, lengths, home, gain.reshape(1, width), q, k, v, u)


def solution(mesh):
    rows = P("seq", "head")
    return jax.shard_map(
        shards,
        mesh=mesh,
        in_specs=(rows, rows, rows, rows, P("head"), P("head"), P(), P("seq")),
        out_specs=(rows, rows, rows),
        check_vma=False,
    )
```

```python
import functools

import jax
import jax.numpy as jnp
from jax import lax
from jax.experimental import pallas as pl
from jax.experimental.pallas import tpu as pltpu
from jax.sharding import PartitionSpec as P

HEAD = 128
GROUP = 128
RING = 4
CHUNK = 4
UNROLL = 8
EPSILON = 1e-06
MESH = pl.DeviceIdType.MESH
F32 = jnp.float32
BF16 = jnp.bfloat16
I32 = jnp.int32
NN = ((1,), (0,))
NT = ((1,), (1,))
TN = ((0,), (0,))


def dot(a, b, dims):
    return lax.dot_general(a, b, (dims, ((), ())), preferred_element_type=F32)


def cols_of(h):
    return slice(h * HEAD, (h + 1) * HEAD)


def iota(shape, dim):
    return lax.broadcasted_iota(I32, shape, dim)


def torus_offsets(ring):
    offsets = [(dy, dz) for dy in range(ring) for dz in range(ring) if (dy, dz) != (0, 0)]
    return sorted(offsets, key=lambda o: min(o[0], ring - o[0]) + min(o[1], ring - o[1]))


def wait_bytes(ref, sem):
    pltpu.make_async_copy(ref, ref, sem).wait()


def fused_kernel(
    heads, groups, devices, sides, docs,
    rate_hbm, len_hbm, home_hbm, gain_hbm, q_hbm, k_hbm, v_hbm, u_hbm,
    qout_ref, kout_ref, vout_ref,
    rate_ref, len_ref, home_ref, gain_ref, arg_sem,
    q_ref, k_ref, v_ref, u_ref, send_ref, got1a_ref, got1b_ref, got2a_ref, got2b_ref, seq_ref, back_ref, prev_ref, after_ref,
    att_ref, vgp_ref, mix_ref,
    dec_ref, qdec_ref, kdec_ref, segr_ref, bef_ref, last_ref, segc_ref,
    hmine_ref, hall_ref, hcomp_ref, order_ref, carry_ref, homes_s, order_s, carry_s,
    mine_ref, gsum_ref,
    kv_sem, qu_sem, own_sem, smem_sem, hsend, hrecv, send1, recv1, send2, recv2a, recv2b,
    send3, recv3, send4, recv4a, recv4b, ssend, srecv,
):
    me = lax.axis_index("seq")
    side = lax.axis_index("head")
    y, z = me // RING, lax.rem(me, RING)
    peers = [lax.rem(y + dy, RING) * RING + lax.rem(z + dz, RING) for dy, dz in torus_offsets(RING)]
    mates = [lax.rem(side + n, sides) for n in range(1, sides)]
    got1_ref, got2_ref = (got1a_ref, got1b_ref), (got2a_ref, got2b_ref)
    others = devices - 1
    total = devices * groups
    chunks = groups // CHUNK
    slab = CHUNK * GROUP
    part = HEAD // RING // 2

    small = [
        pltpu.make_async_copy(src, dst, arg_sem.at[n])
        for n, (src, dst) in enumerate(
            [(rate_hbm, rate_ref), (len_hbm, len_ref), (home_hbm, home_ref), (gain_hbm, gain_ref)]
        )
    ]
    for copy in small:
        copy.start()
    barrier = pltpu.get_barrier_semaphore()
    for peer in peers:
        pl.semaphore_signal(barrier, inc=1, device_id=(peer, side), device_id_type=MESH)
    for mate in mates:
        pl.semaphore_signal(barrier, inc=1, device_id=(me, mate), device_id_type=MESH)

    def slab_copy(hbm, ref, c, sem):
        rows = pl.ds(c * slab, slab)
        return pltpu.make_async_copy(hbm.at[rows], ref.at[rows], sem)

    for c in range(chunks):
        slab_copy(k_hbm, k_ref, c, kv_sem.at[0, c]).start()
        slab_copy(v_hbm, v_ref, c, kv_sem.at[1, c]).start()
    load_q = pltpu.make_async_copy(q_hbm, q_ref, qu_sem.at[0])
    load_u = pltpu.make_async_copy(u_hbm, u_ref, qu_sem.at[1])
    load_q.start()
    load_u.start()

    for copy in small:
        copy.wait()
    row = iota((GROUP, GROUP), 0).astype(F32)
    spread = row - iota((GROUP, GROUP), 1).astype(F32)
    for h in range(heads):
        r = rate_ref[h]
        dec_ref[h] = jnp.where(spread >= 0.0, jnp.exp(-r * jnp.maximum(spread, 0.0)), 0.0)
        qdec_ref[h] = jnp.exp(-r * (row + 1.0))
        kdec_ref[h] = jnp.exp(-r * (GROUP - 1.0 - row))

    home_rows = jnp.zeros((groups, HEAD), I32)
    home_lanes = jnp.zeros((8, HEAD), I32)
    group_row = iota((groups, HEAD), 0)
    lane8 = iota((8, HEAD), 1)
    for i in range(groups):
        home_rows = jnp.where(group_row == i, home_ref[i], home_rows)
        home_lanes = jnp.where(lane8 == i, home_ref[i], home_lanes)
    hmine_ref[...] = home_lanes
    hall_ref[me] = home_lanes
    steps = iota((8, HEAD), 0) * HEAD + lane8
    pos = home_rows * GROUP + iota((groups, HEAD), 1)
    pos_b = home_rows * GROUP - 1
    step_b = steps * GROUP - 1
    seg = jnp.zeros_like(pos)
    seg_b = jnp.zeros_like(pos)
    step_seg_b = jnp.zeros_like(steps)
    step_seg_e = jnp.zeros_like(steps)
    end = jnp.int32(0)
    for n in range(docs):
        end = end + len_ref[n]
        seg += (pos >= end).astype(I32)
        seg_b += (pos_b >= end).astype(I32)
        step_seg_b += (step_b >= end).astype(I32)
        step_seg_e += (step_b + GROUP >= end).astype(I32)
    seg_b = jnp.where(home_rows == 0, -1, seg_b).astype(F32)
    seg = seg.astype(F32)
    for i in range(groups):
        segr_ref[i] = seg[i : i + 1]
        bef_ref[i] = seg_b[i : i + 1]
        last_ref[i] = jnp.broadcast_to(seg[i : i + 1, GROUP - 1 :], (1, HEAD))
    own_rate = rate_ref[me // RING]
    keep = jnp.exp(jnp.zeros((8, HEAD), F32) - own_rate * GROUP)
    joined = (step_seg_b == step_seg_e) | (steps == 0)
    carry_ref[...] = jnp.where(joined, keep, 0.0)
    carry_copy = pltpu.make_async_copy(carry_ref, carry_s, smem_sem.at[0])
    carry_copy.start()

    pl.semaphore_wait(barrier, others + sides - 1)
    for peer in peers:
        pltpu.make_async_remote_copy(
            src_ref=hmine_ref, dst_ref=hall_ref.at[me], send_sem=hsend, recv_sem=hrecv,
            device_id=(peer, side), device_id_type=MESH,
        ).start()

    def rows_of(i):
        return pl.ds(pl.multiple_of(i * GROUP, GROUP), GROUP)

    def scatter(got_ref, half, c, send_sem, recv_sem):
        for peer in peers:
            pltpu.make_async_remote_copy(
                src_ref=send_ref.at[half, peer, pl.ds(c * CHUNK, CHUNK)],
                dst_ref=got_ref[half].at[pl.ds(me * groups + c * CHUNK, CHUNK)],
                send_sem=send_sem, recv_sem=recv_sem.at[half],
                device_id=(peer, side), device_id_type=MESH,
            ).start()

    def give_back(dst_ref, half, start, size, send_sem, recv_sem):
        for peer in peers:
            pltpu.make_async_remote_copy(
                src_ref=back_ref.at[half, pl.ds(peer * groups + start, size)],
                dst_ref=dst_ref.at[half, me, pl.ds(start, size)],
                send_sem=send_sem, recv_sem=recv_sem,
                device_id=(peer, side), device_id_type=MESH,
            ).start()

    def own_slice(got_ref, half, n):
        return pltpu.make_async_copy(
            send_ref.at[half, me], got_ref[half].at[pl.ds(me * groups, groups)], own_sem.at[n, half]
        )

    def own_back(dst_ref, half, n):
        return pltpu.make_async_copy(
            back_ref.at[half, pl.ds(me * groups, groups)], dst_ref.at[half, me], own_sem.at[n, half]
        )

    def store_state(i, h, s):
        send_ref[:, RING * h : RING * (h + 1), i] = s.astype(BF16).reshape(2, RING, part, HEAD)

    def state_of(ref, i, h):
        return ref[:, RING * h : RING * (h + 1), i].reshape(HEAD, HEAD)

    def summary_group(i, _):
        rows = rows_of(i)
        seg_c = jnp.broadcast_to(segr_ref[i], (GROUP, GROUP)).T
        segc_ref[i] = seg_c
        live = seg_c == last_ref[i]
        for h in range(heads):
            cols = cols_of(h)
            w = (jnp.where(live, kdec_ref[h], 0.0) * v_ref[rows, cols].astype(F32)).astype(BF16)
            store_state(i, h, dot(k_ref[rows, cols], w, TN))
        return 0

    def summary_chunk(c, _):
        slab_copy(k_hbm, k_ref, c, kv_sem.at[0, c]).wait()
        slab_copy(v_hbm, v_ref, c, kv_sem.at[1, c]).wait()
        lax.fori_loop(c * CHUNK, (c + 1) * CHUNK, summary_group, 0)
        scatter(got1_ref, 0, c, send1, recv1)
        return 0

    lax.fori_loop(0, chunks, summary_chunk, 0)

    def second_half(c, _):
        scatter(got1_ref, 1, c, send1, recv1)
        return 0

    lax.fori_loop(0, chunks, second_half, 0)
    own_slice(got1_ref, 0, 0).start()
    own_slice(got1_ref, 1, 0).start()

    wait_bytes(hall_ref.at[pl.ds(0, others)], hrecv)
    for d in range(devices):
        hcomp_ref[d : d + 1] = hall_ref[d, 0:1]
    homes_copy = pltpu.make_async_copy(hcomp_ref, homes_s, smem_sem.at[1])
    homes_copy.start()
    homes_copy.wait()

    def invert(b, acc):
        for n in range(UNROLL):
            p = b * UNROLL + n
            acc = jnp.where(steps == homes_s[p // groups, lax.rem(p, groups)], p, acc)
        return acc

    order_ref[...] = lax.fori_loop(0, total // UNROLL, invert, jnp.zeros((8, HEAD), I32))
    order_copy = pltpu.make_async_copy(order_ref, order_s, smem_sem.at[2])
    order_copy.start()
    load_q.wait()
    load_u.wait()

    def inner_group(i, _):
        rows = rows_of(i)
        same = segc_ref[i] == segr_ref[i]
        for h in range(heads):
            cols = cols_of(h)
            scores = dot(q_ref[rows, cols], k_ref[rows, cols], NT)
            mixing = (scores * jnp.where(same, dec_ref[h], 0.0)).astype(BF16)
            mix_ref[i * heads + h] = mixing
            att_ref[rows, cols] = dot(mixing, v_ref[rows, cols], NN)
        return 0

    lax.fori_loop(0, groups, inner_group, 0)
    order_copy.wait()
    carry_copy.wait()

    def scan(got_ref, half, reverse):
        def step(b, state):
            b = total // UNROLL - 1 - b if reverse else b
            for n in range(UNROLL):
                t = b * UNROLL + (UNROLL - 1 - n if reverse else n)
                hi, lo = t // HEAD, lax.rem(t, HEAD)
                seq_ref[t] = state.astype(BF16)
                state = carry_s[hi, lo] * state + got_ref[half][order_s[hi, lo]].astype(F32)
            return state

        lax.fori_loop(0, total // UNROLL, step, jnp.zeros((part, HEAD), F32))

        def put(b, _):
            for n in range(UNROLL):
                p = b * UNROLL + n
                back_ref[half, p] = seq_ref[homes_s[p // groups, lax.rem(p, groups)]]
            return 0

        lax.fori_loop(0, total // UNROLL, put, 0)

    half_groups = groups // 2

    def turn(got_ref, dst_ref, n, reverse, recv_sem, send_back, recv_first, recv_second):
        own_slice(got_ref, 0, n).wait()
        wait_bytes(got_ref[0].at[pl.ds(0, others * groups)], recv_sem.at[0])
        scan(got_ref, 0, reverse)
        give_back(dst_ref, 0, 0, half_groups, send_back, recv_first.at[0])
        own_back(dst_ref, 0, n + 1).start()
        own_slice(got_ref, 1, n).wait()
        wait_bytes(got_ref[1].at[pl.ds(0, others * groups)], recv_sem.at[1])
        scan(got_ref, 1, reverse)
        own_back(dst_ref, 1, n + 1).start()

        def rest(c, _):
            @pl.when(c == chunks // 2)
            def _():
                give_back(dst_ref, 0, half_groups, half_groups, send_back, recv_first.at[1])

            give_back(dst_ref, 1, c * CHUNK, CHUNK, send_back, recv_second.at[c])
            return 0

        lax.fori_loop(0, chunks, rest, 0)

    def turned(dst_ref, c, recv_first, recv_second):
        @pl.when(lax.rem(c, chunks // 2) == 0)
        def _():
            wait_bytes(
                dst_ref.at[0, pl.ds(0, others), pl.ds(0, half_groups)], recv_first.at[c // (chunks // 2)]
            )

        wait_bytes(dst_ref.at[1, pl.ds(0, others), pl.ds(0, CHUNK)], recv_second.at[c])

    def sent(sem):
        wait_bytes(send_ref.at[0, pl.ds(0, others)], sem)
        wait_bytes(send_ref.at[0, pl.ds(0, others)], sem)

    turn(got1_ref, prev_ref, 0, False, recv1, send2, recv2a, recv2b)
    sent(send1)
    wait_bytes(hall_ref.at[pl.ds(0, others)], hsend)
    own_back(prev_ref, 0, 1).wait()
    own_back(prev_ref, 1, 1).wait()

    lane = iota((GROUP, HEAD), 1)
    pieces = GROUP // (2 * CHUNK)
    width = 2 * CHUNK

    def output_group(c, g, acc):
        i = c * CHUNK + g
        rows = rows_of(i)
        live = segc_ref[i] == bef_ref[i]
        squares = jnp.zeros((GROUP, HEAD), F32)
        crossed = jnp.zeros((GROUP, HEAD), F32)
        for h in range(heads):
            cols = cols_of(h)
            carried = dot(q_ref[rows, cols], state_of(prev_ref, i, h), NN)
            out = att_ref[rows, cols] + jnp.where(live, qdec_ref[h], 0.0) * carried
            att_ref[rows, cols] = out
            squares += out * out
            crossed += gain_ref[:, cols] * u_ref[rows, cols].astype(F32) * out
        squares = jnp.sum(squares, axis=1, keepdims=True)
        crossed = jnp.sum(crossed, axis=1, keepdims=True)
        return jnp.where(lane == g, squares, jnp.where(lane == g + CHUNK, crossed, acc))

    def total_copy(c, n):
        return pltpu.make_async_remote_copy(
            src_ref=mine_ref.at[c], dst_ref=gsum_ref.at[c, n], send_sem=ssend.at[c], recv_sem=srecv.at[c],
            device_id=(me, mates[n]), device_id_type=MESH,
        )

    def output_chunk(c):
        turned(prev_ref, c, recv2a, recv2b)
        acc = lax.fori_loop(0, CHUNK, functools.partial(output_group, c), jnp.zeros((GROUP, HEAD), F32))
        packed = acc[0:width]
        for n in range(1, pieces):
            packed += pltpu.roll(acc[n * width : (n + 1) * width], n * width, 1)
        mine_ref[c] = packed
        for n in range(sides - 1):
            total_copy(c, n).start()

    channels = heads * HEAD * sides

    def cotangent_group(c, sums, g, _):
        i = c * CHUNK + g
        rows = rows_of(i)
        live = segc_ref[i] == bef_ref[i]
        squares = jnp.sum(jnp.where(lane == g, sums, 0.0), axis=1, keepdims=True)
        crossed = jnp.sum(jnp.where(lane == g + CHUNK, sums, 0.0), axis=1, keepdims=True)
        scaling = lax.rsqrt(squares / channels + EPSILON)
        pull = scaling * scaling * scaling * (crossed / channels)
        for h in range(heads):
            cols = cols_of(h)
            wide = gain_ref[:, cols] * u_ref[rows, cols].astype(F32)
            grad = (scaling * wide - pull * att_ref[rows, cols]).astype(BF16)
            u_ref[rows, cols] = grad
            w = (jnp.where(live, qdec_ref[h], 0.0) * grad.astype(F32)).astype(BF16)
            store_state(i, h, dot(q_ref[rows, cols], w, TN))
        return 0

    def cotangent_chunk(c):
        wait_bytes(gsum_ref.at[c], srecv.at[c])
        wait_bytes(gsum_ref.at[c], ssend.at[c])
        both = mine_ref[c]
        for n in range(sides - 1):
            both += gsum_ref[c, n]
        sums = jnp.concatenate(
            [both] + [pltpu.roll(both, HEAD - n * width, 1) for n in range(1, pieces)], axis=0
        )
        lax.fori_loop(0, CHUNK, functools.partial(cotangent_group, c, sums), 0)
        scatter(got2_ref, 0, c, send3, recv3)

        @pl.when(c < chunks - 2)
        def _():
            scatter(got2_ref, 1, c, send3, recv3)

    def middle(c, _):
        @pl.when(c < chunks)
        def _():
            output_chunk(c)

        @pl.when(c >= 1)
        def _():
            cotangent_chunk(c - 1)

        return 0

    lax.fori_loop(0, chunks + 1, middle, 0)
    for c in (chunks - 2, chunks - 1):
        scatter(got2_ref, 1, c, send3, recv3)
    own_slice(got2_ref, 0, 2).start()
    own_slice(got2_ref, 1, 2).start()

    def local_group(i, _):
        rows = rows_of(i)
        seg_c = segc_ref[i]
        same = seg_c == segr_ref[i]
        live = seg_c == bef_ref[i]
        for h in range(heads):
            cols = cols_of(h)
            g, k, q = u_ref[rows, cols], k_ref[rows, cols], q_ref[rows, cols]
            score = (dot(g, v_ref[rows, cols], NT) * jnp.where(same, dec_ref[h], 0.0)).astype(BF16)
            carried = jnp.where(live, qdec_ref[h], 0.0) * dot(g, state_of(prev_ref, i, h), NT)
            qout_ref[rows, cols] = (dot(score, k, NN) + carried).astype(BF16)
            att_ref[rows, cols] = dot(score, q, TN)
            vgp_ref[rows, cols] = dot(mix_ref[i * heads + h], g, TN)
        return 0

    early = groups // 2
    lax.fori_loop(0, early, local_group, 0)
    sent(send2)
    turn(got2_ref, after_ref, 2, True, recv3, send4, recv4a, recv4b)
    lax.fori_loop(early, groups, local_group, 0)
    own_back(after_ref, 0, 3).wait()
    own_back(after_ref, 1, 3).wait()

    def final_group(i, _):
        rows = rows_of(i)
        live = segc_ref[i] == last_ref[i]
        for h in range(heads):
            cols = cols_of(h)
            after = state_of(after_ref, i, h)
            w = jnp.where(live, kdec_ref[h], 0.0)
            kout_ref[rows, cols] = (att_ref[rows, cols] + w * dot(v_ref[rows, cols], after, NT)).astype(BF16)
            vout_ref[rows, cols] = (vgp_ref[rows, cols] + w * dot(k_ref[rows, cols], after, NN)).astype(BF16)
        return 0

    def final_chunk(c, _):
        turned(after_ref, c, recv4a, recv4b)
        lax.fori_loop(c * CHUNK, (c + 1) * CHUNK, final_group, 0)
        return 0

    lax.fori_loop(0, chunks, final_chunk, 0)
    sent(send3)
    sent(send4)


def store_kernel(a_ref, b_ref, c_ref, ao_ref, bo_ref, co_ref, sem):
    pairs = ((a_ref, ao_ref), (b_ref, bo_ref), (c_ref, co_ref))
    copies = [pltpu.make_async_copy(src, dst, sem.at[n]) for n, (src, dst) in enumerate(pairs)]
    for copy in copies:
        copy.start()
    for copy in copies:
        copy.wait()


def shards(q, k, v, u, gain, rate, lengths, home):
    devices = lax.axis_size("seq")
    sides = lax.axis_size("head")
    heads = q.shape[1] // HEAD
    groups = home.shape[0]
    rows, width = q.shape
    docs = lengths.shape[0]
    total = devices * groups
    chunks = groups // CHUNK
    part = HEAD // RING // 2
    any_ = pl.BlockSpec(memory_space=pl.ANY)
    vmem, dma = pltpu.VMEM, pltpu.SemaphoreType.DMA
    table = vmem((heads, GROUP, GROUP), F32)
    strip = vmem((groups, 1, HEAD), F32)
    token = vmem((rows, width), BF16)
    flat = vmem((total, part, HEAD), BF16)
    state = vmem((2, devices, groups, part, HEAD), BF16)
    wide = vmem((rows, width), F32)
    scratch = (
        [pltpu.SMEM((heads,), F32), pltpu.SMEM((docs,), I32), pltpu.SMEM((groups,), I32)]
        + [vmem((1, width), F32), dma((4,))]
        + [token] * 4 + [state] + [flat] * 5 + [vmem((2, total, part, HEAD), BF16), state, state]
        + [wide, wide, vmem((groups * heads, GROUP, GROUP), BF16)]
        + [table] * 3 + [strip] * 3 + [vmem((groups, GROUP, GROUP), F32)]
        + [vmem((8, HEAD), I32), vmem((devices, 8, HEAD), I32), vmem((devices, HEAD), I32)]
        + [vmem((8, HEAD), I32), vmem((8, HEAD), F32)]
        + [pltpu.SMEM((devices, HEAD), I32), pltpu.SMEM((8, HEAD), I32), pltpu.SMEM((8, HEAD), F32)]
        + [vmem((chunks, 2 * CHUNK, HEAD), F32), vmem((chunks, sides - 1, 2 * CHUNK, HEAD), F32)]
        + [dma((2, chunks)), dma((2,)), dma((4, 2)), dma((3,)), dma, dma]
        + [dma, dma((2,)), dma, dma((2,)), dma((chunks,))] * 2
        + [dma((chunks,)), dma((chunks,))]
    )
    grads = pl.pallas_call(
        functools.partial(fused_kernel, heads, groups, devices, sides, docs),
        out_shape=(pltpu.VMEM((rows, width), BF16),) * 3,
        in_specs=[any_] * 8,
        out_specs=(pl.BlockSpec(memory_space=vmem),) * 3,
        scratch_shapes=scratch,
        compiler_params=pltpu.CompilerParams(
            collective_id=0, has_side_effects=True, vmem_limit_bytes=50 << 20
        ),
    )(rate, lengths, home, gain.reshape(1, width), q, k, v, u)
    return pl.pallas_call(
        store_kernel,
        out_shape=(jax.ShapeDtypeStruct((rows, width), BF16),) * 3,
        in_specs=[pl.BlockSpec(memory_space=vmem)] * 3,
        out_specs=(any_,) * 3,
        scratch_shapes=[dma((3,))],
        compiler_params=pltpu.CompilerParams(vmem_limit_bytes=4 << 20),
    )(*[pltpu.with_memory_space_constraint(g, vmem) for g in grads])


def solution(mesh):
    rows = P("seq", "head")
    return jax.shard_map(
        shards,
        mesh=mesh,
        in_specs=(rows, rows, rows, rows, P("head"), P("head"), P(), P("seq")),
        out_specs=(rows, rows, rows),
        check_vma=False,
    )
```

```python
import functools

import jax
import jax.numpy as jnp
from jax import lax
from jax.experimental import pallas as pl
from jax.experimental.pallas import tpu as pltpu
from jax.sharding import PartitionSpec as P

HEAD = 128
GROUP = 128
RING = 4
CHUNK = 4
UNROLL = 8
STEPS = 16
EPSILON = 1e-06
MESH = pl.DeviceIdType.MESH
F32 = jnp.float32
BF16 = jnp.bfloat16
I32 = jnp.int32
NN = ((1,), (0,))
NT = ((1,), (1,))
TN = ((0,), (0,))


def dot(a, b, dims):
    return lax.dot_general(a, b, (dims, ((), ())), preferred_element_type=F32)


def cols_of(h):
    return slice(h * HEAD, (h + 1) * HEAD)


def iota(shape, dim):
    return lax.broadcasted_iota(I32, shape, dim)


def torus_offsets(ring):
    offsets = [(dy, dz) for dy in range(ring) for dz in range(ring) if (dy, dz) != (0, 0)]
    return sorted(offsets, key=lambda o: min(o[0], ring - o[0]) + min(o[1], ring - o[1]))


def wait_bytes(ref, sem):
    pltpu.make_async_copy(ref, ref, sem).wait()


def fused_kernel(
    heads, groups, devices, sides, docs,
    rate_hbm, len_hbm, home_hbm, gain_hbm, q_hbm, k_hbm, v_hbm, u_hbm,
    qout_ref, kout_ref, vout_ref,
    rate_ref, len_ref, home_ref, gain_ref, arg_sem,
    q_ref, k_ref, v_ref, u_ref, send_ref, got1a_ref, got1b_ref, got2a_ref, got2b_ref, seq_ref, back_ref, prev_ref, after_ref,
    att_ref, vgp_ref, mix_ref,
    dec_ref, qdec_ref, kdec_ref, segr_ref, bef_ref, last_ref, segc_ref,
    hmine_ref, hall_ref, hcomp_ref, order_ref, carry_ref, homes_s, order_s, carry_s,
    mine_ref, gsum_ref,
    kv_sem, qu_sem, own_sem, smem_sem, hsend, hrecv, send1, recv1, send2, recv2a, recv2b,
    send3, recv3, send4, recv4a, recv4b, ssend, srecv,
):
    me = lax.axis_index("seq")
    side = lax.axis_index("head")
    y, z = me // RING, lax.rem(me, RING)
    peers = [lax.rem(y + dy, RING) * RING + lax.rem(z + dz, RING) for dy, dz in torus_offsets(RING)]
    mates = [lax.rem(side + n, sides) for n in range(1, sides)]
    got1_ref, got2_ref = (got1a_ref, got1b_ref), (got2a_ref, got2b_ref)
    others = devices - 1
    total = devices * groups
    chunks = groups // CHUNK
    slab = CHUNK * GROUP
    part = HEAD // RING // 2

    small = [
        pltpu.make_async_copy(src, dst, arg_sem.at[n])
        for n, (src, dst) in enumerate(
            [(rate_hbm, rate_ref), (len_hbm, len_ref), (home_hbm, home_ref), (gain_hbm, gain_ref)]
        )
    ]
    for copy in small:
        copy.start()
    barrier = pltpu.get_barrier_semaphore()
    for peer in peers:
        pl.semaphore_signal(barrier, inc=1, device_id=(peer, side), device_id_type=MESH)
    for mate in mates:
        pl.semaphore_signal(barrier, inc=1, device_id=(me, mate), device_id_type=MESH)

    def slab_copy(hbm, ref, c, sem):
        rows = pl.ds(c * slab, slab)
        return pltpu.make_async_copy(hbm.at[rows], ref.at[rows], sem)

    for c in range(chunks):
        slab_copy(k_hbm, k_ref, c, kv_sem.at[0, c]).start()
        slab_copy(v_hbm, v_ref, c, kv_sem.at[1, c]).start()
    load_q = pltpu.make_async_copy(q_hbm, q_ref, qu_sem.at[0])
    load_u = pltpu.make_async_copy(u_hbm, u_ref, qu_sem.at[1])

    for copy in small:
        copy.wait()
    row = iota((GROUP, GROUP), 0).astype(F32)
    for h in range(heads):
        kdec_ref[h] = jnp.exp(-rate_ref[h] * (GROUP - 1.0 - row))

    home_rows = jnp.zeros((groups, HEAD), I32)
    home_lanes = jnp.zeros((8, HEAD), I32)
    group_row = iota((groups, HEAD), 0)
    lane8 = iota((8, HEAD), 1)
    for i in range(groups):
        home_rows = jnp.where(group_row == i, home_ref[i], home_rows)
        home_lanes = jnp.where(lane8 == i, home_ref[i], home_lanes)
    hmine_ref[...] = home_lanes
    hall_ref[me] = home_lanes
    steps = iota((8, HEAD), 0) * HEAD + lane8
    pos = home_rows * GROUP + iota((groups, HEAD), 1)
    pos_b = home_rows * GROUP - 1
    step_b = steps * GROUP - 1
    seg = jnp.zeros_like(pos)
    seg_b = jnp.zeros_like(pos)
    step_seg_b = jnp.zeros_like(steps)
    step_seg_e = jnp.zeros_like(steps)
    end = jnp.int32(0)
    for n in range(docs):
        end = end + len_ref[n]
        seg += (pos >= end).astype(I32)
        seg_b += (pos_b >= end).astype(I32)
        step_seg_b += (step_b >= end).astype(I32)
        step_seg_e += (step_b + GROUP >= end).astype(I32)
    seg_b = jnp.where(home_rows == 0, -1, seg_b).astype(F32)
    seg = seg.astype(F32)
    for i in range(groups):
        segr_ref[i] = seg[i : i + 1]
        bef_ref[i] = seg_b[i : i + 1]
        last_ref[i] = jnp.broadcast_to(seg[i : i + 1, GROUP - 1 :], (1, HEAD))
    own_rate = rate_ref[me // RING]
    keep = jnp.exp(jnp.zeros((8, HEAD), F32) - own_rate * GROUP)
    joined = (step_seg_b == step_seg_e) | (steps == 0)
    carry_ref[...] = jnp.where(joined, keep, 0.0)
    carry_copy = pltpu.make_async_copy(carry_ref, carry_s, smem_sem.at[0])
    carry_copy.start()

    pl.semaphore_wait(barrier, others + sides - 1)
    load_q.start()
    load_u.start()

    def rows_of(i):
        return pl.ds(pl.multiple_of(i * GROUP, GROUP), GROUP)

    def scatter(got_ref, half, c, send_sem, recv_sem):
        for peer in peers:
            pltpu.make_async_remote_copy(
                src_ref=send_ref.at[half, peer, pl.ds(c * CHUNK, CHUNK)],
                dst_ref=got_ref[half].at[pl.ds(me * groups + c * CHUNK, CHUNK)],
                send_sem=send_sem, recv_sem=recv_sem.at[half],
                device_id=(peer, side), device_id_type=MESH,
            ).start()

    def give_back(dst_ref, half, start, size, send_sem, recv_sem):
        for peer in peers:
            pltpu.make_async_remote_copy(
                src_ref=back_ref.at[half, pl.ds(peer * groups + start, size)],
                dst_ref=dst_ref.at[half, me, pl.ds(start, size)],
                send_sem=send_sem, recv_sem=recv_sem,
                device_id=(peer, side), device_id_type=MESH,
            ).start()

    def own_slice(got_ref, half, n):
        return pltpu.make_async_copy(
            send_ref.at[half, me], got_ref[half].at[pl.ds(me * groups, groups)], own_sem.at[n, half]
        )

    def own_back(dst_ref, half, n):
        return pltpu.make_async_copy(
            back_ref.at[half, pl.ds(me * groups, groups)], dst_ref.at[half, me], own_sem.at[n, half]
        )

    def store_state(i, h, s):
        send_ref[:, RING * h : RING * (h + 1), i] = s.astype(BF16).reshape(2, RING, part, HEAD)

    def state_of(ref, i, h):
        return ref[:, RING * h : RING * (h + 1), i].reshape(HEAD, HEAD)

    def summary_group(i, _):
        rows = rows_of(i)
        seg_c = jnp.broadcast_to(segr_ref[i], (GROUP, GROUP)).T
        segc_ref[i] = seg_c
        live = seg_c == last_ref[i]
        for h in range(heads):
            cols = cols_of(h)
            w = (jnp.where(live, kdec_ref[h], 0.0) * v_ref[rows, cols].astype(F32)).astype(BF16)
            store_state(i, h, dot(k_ref[rows, cols], w, TN))
        return 0

    def summary_chunk(c, _):
        slab_copy(k_hbm, k_ref, c, kv_sem.at[0, c]).wait()
        slab_copy(v_hbm, v_ref, c, kv_sem.at[1, c]).wait()
        lax.fori_loop(c * CHUNK, (c + 1) * CHUNK, summary_group, 0)
        scatter(got1_ref, 0, c, send1, recv1)
        return 0

    summary_chunk(0, 0)
    for peer in peers:
        pltpu.make_async_remote_copy(
            src_ref=hmine_ref, dst_ref=hall_ref.at[me], send_sem=hsend, recv_sem=hrecv,
            device_id=(peer, side), device_id_type=MESH,
        ).start()
    lax.fori_loop(1, chunks, summary_chunk, 0)

    def second_half(c, _):
        scatter(got1_ref, 1, c, send1, recv1)
        return 0

    lax.fori_loop(0, chunks, second_half, 0)
    own_slice(got1_ref, 0, 0).start()
    own_slice(got1_ref, 1, 0).start()

    spread = row - iota((GROUP, GROUP), 1).astype(F32)
    for h in range(heads):
        r = rate_ref[h]
        dec_ref[h] = jnp.where(spread >= 0.0, jnp.exp(-r * jnp.maximum(spread, 0.0)), 0.0)
        qdec_ref[h] = jnp.exp(-r * (row + 1.0))

    wait_bytes(hall_ref.at[pl.ds(0, others)], hrecv)
    for d in range(devices):
        hcomp_ref[d : d + 1] = hall_ref[d, 0:1]
    homes_copy = pltpu.make_async_copy(hcomp_ref, homes_s, smem_sem.at[1])
    homes_copy.start()
    homes_copy.wait()

    def invert(b, acc):
        for n in range(UNROLL):
            p = b * UNROLL + n
            acc = jnp.where(steps == homes_s[p // groups, lax.rem(p, groups)], p, acc)
        return acc

    order_ref[...] = lax.fori_loop(0, total // UNROLL, invert, jnp.zeros((8, HEAD), I32))
    order_copy = pltpu.make_async_copy(order_ref, order_s, smem_sem.at[2])
    order_copy.start()
    load_q.wait()
    load_u.wait()

    def inner_group(i, _):
        rows = rows_of(i)
        same = segc_ref[i] == segr_ref[i]
        for h in range(heads):
            cols = cols_of(h)
            scores = dot(q_ref[rows, cols], k_ref[rows, cols], NT)
            mixing = (scores * jnp.where(same, dec_ref[h], 0.0)).astype(BF16)
            mix_ref[i * heads + h] = mixing
            att_ref[rows, cols] = dot(mixing, v_ref[rows, cols], NN)
        return 0

    lax.fori_loop(0, groups, inner_group, 0)
    order_copy.wait()
    carry_copy.wait()

    def scan(got_ref, half, reverse):
        def step(b, state):
            base = (total // STEPS - 1 - b if reverse else b) * STEPS
            hi, lo = base // HEAD, lax.rem(base, HEAD)
            arrived = [got_ref[half][order_s[hi, lo + n]] for n in range(STEPS)]
            keeps = [carry_s[hi, lo + n] for n in range(STEPS)]
            states = [None] * STEPS
            for n in range(STEPS):
                n = STEPS - 1 - n if reverse else n
                states[n] = state.astype(BF16)
                state = keeps[n] * state + arrived[n].astype(F32)
            for n in range(STEPS):
                seq_ref[base + n] = states[n]
            return state

        lax.fori_loop(0, total // STEPS, step, jnp.zeros((part, HEAD), F32))

        def put(d, _):
            found = [seq_ref[homes_s[d, n]] for n in range(groups)]
            for n in range(groups):
                back_ref[half, d * groups + n] = found[n]
            return 0

        lax.fori_loop(0, devices, put, 0)

    half_groups = groups // 2

    def turn(got_ref, dst_ref, n, reverse, recv_sem, send_back, recv_first, recv_second):
        own_slice(got_ref, 0, n).wait()
        wait_bytes(got_ref[0].at[pl.ds(0, others * groups)], recv_sem.at[0])
        scan(got_ref, 0, reverse)
        give_back(dst_ref, 0, 0, half_groups, send_back, recv_first.at[0])
        own_back(dst_ref, 0, n + 1).start()
        own_slice(got_ref, 1, n).wait()
        wait_bytes(got_ref[1].at[pl.ds(0, others * groups)], recv_sem.at[1])
        scan(got_ref, 1, reverse)
        own_back(dst_ref, 1, n + 1).start()

        def rest(c, _):
            @pl.when(c == chunks // 2)
            def _():
                give_back(dst_ref, 0, half_groups, half_groups, send_back, recv_first.at[1])

            give_back(dst_ref, 1, c * CHUNK, CHUNK, send_back, recv_second.at[c])
            return 0

        lax.fori_loop(0, chunks, rest, 0)

    def turned(dst_ref, c, recv_first, recv_second):
        @pl.when(lax.rem(c, chunks // 2) == 0)
        def _():
            wait_bytes(
                dst_ref.at[0, pl.ds(0, others), pl.ds(0, half_groups)], recv_first.at[c // (chunks // 2)]
            )

        wait_bytes(dst_ref.at[1, pl.ds(0, others), pl.ds(0, CHUNK)], recv_second.at[c])

    def sent(sem):
        wait_bytes(send_ref.at[0, pl.ds(0, others)], sem)
        wait_bytes(send_ref.at[0, pl.ds(0, others)], sem)

    turn(got1_ref, prev_ref, 0, False, recv1, send2, recv2a, recv2b)
    sent(send1)
    wait_bytes(hall_ref.at[pl.ds(0, others)], hsend)
    own_back(prev_ref, 0, 1).wait()
    own_back(prev_ref, 1, 1).wait()

    lane = iota((GROUP, HEAD), 1)
    pieces = GROUP // (2 * CHUNK)
    width = 2 * CHUNK

    def output_group(c, g, acc):
        i = c * CHUNK + g
        rows = rows_of(i)
        live = segc_ref[i] == bef_ref[i]
        squares = jnp.zeros((GROUP, HEAD), F32)
        crossed = jnp.zeros((GROUP, HEAD), F32)
        for h in range(heads):
            cols = cols_of(h)
            carried = dot(q_ref[rows, cols], state_of(prev_ref, i, h), NN)
            out = att_ref[rows, cols] + jnp.where(live, qdec_ref[h], 0.0) * carried
            att_ref[rows, cols] = out
            squares += out * out
            crossed += gain_ref[:, cols] * u_ref[rows, cols].astype(F32) * out
        squares = jnp.sum(squares, axis=1, keepdims=True)
        crossed = jnp.sum(crossed, axis=1, keepdims=True)
        return jnp.where(lane == g, squares, jnp.where(lane == g + CHUNK, crossed, acc))

    def total_copy(c, n):
        return pltpu.make_async_remote_copy(
            src_ref=mine_ref.at[c], dst_ref=gsum_ref.at[c, n], send_sem=ssend.at[c], recv_sem=srecv.at[c],
            device_id=(me, mates[n]), device_id_type=MESH,
        )

    def output_chunk(c):
        turned(prev_ref, c, recv2a, recv2b)
        acc = lax.fori_loop(0, CHUNK, functools.partial(output_group, c), jnp.zeros((GROUP, HEAD), F32))
        packed = acc[0:width]
        for n in range(1, pieces):
            packed += pltpu.roll(acc[n * width : (n + 1) * width], n * width, 1)
        mine_ref[c] = packed
        for n in range(sides - 1):
            total_copy(c, n).start()

    channels = heads * HEAD * sides

    def cotangent_group(c, sums, g, _):
        i = c * CHUNK + g
        rows = rows_of(i)
        live = segc_ref[i] == bef_ref[i]
        squares = jnp.sum(jnp.where(lane == g, sums, 0.0), axis=1, keepdims=True)
        crossed = jnp.sum(jnp.where(lane == g + CHUNK, sums, 0.0), axis=1, keepdims=True)
        scaling = lax.rsqrt(squares / channels + EPSILON)
        pull = scaling * scaling * scaling * (crossed / channels)
        for h in range(heads):
            cols = cols_of(h)
            wide = gain_ref[:, cols] * u_ref[rows, cols].astype(F32)
            grad = (scaling * wide - pull * att_ref[rows, cols]).astype(BF16)
            u_ref[rows, cols] = grad
            w = (jnp.where(live, qdec_ref[h], 0.0) * grad.astype(F32)).astype(BF16)
            store_state(i, h, dot(q_ref[rows, cols], w, TN))
        return 0

    def cotangent_chunk(c):
        wait_bytes(gsum_ref.at[c], srecv.at[c])
        wait_bytes(gsum_ref.at[c], ssend.at[c])
        both = mine_ref[c]
        for n in range(sides - 1):
            both += gsum_ref[c, n]
        sums = jnp.concatenate(
            [both] + [pltpu.roll(both, HEAD - n * width, 1) for n in range(1, pieces)], axis=0
        )
        lax.fori_loop(0, CHUNK, functools.partial(cotangent_group, c, sums), 0)
        scatter(got2_ref, 0, c, send3, recv3)

        @pl.when(c < chunks - 2)
        def _():
            scatter(got2_ref, 1, c, send3, recv3)

    def middle(c, _):
        @pl.when(c < chunks)
        def _():
            output_chunk(c)

        @pl.when(c >= 1)
        def _():
            cotangent_chunk(c - 1)

        return 0

    lax.fori_loop(0, chunks + 1, middle, 0)
    for c in (chunks - 2, chunks - 1):
        scatter(got2_ref, 1, c, send3, recv3)
    own_slice(got2_ref, 0, 2).start()
    own_slice(got2_ref, 1, 2).start()

    def local_group(i, _):
        rows = rows_of(i)
        seg_c = segc_ref[i]
        same = seg_c == segr_ref[i]
        live = seg_c == bef_ref[i]
        for h in range(heads):
            cols = cols_of(h)
            g, k, q = u_ref[rows, cols], k_ref[rows, cols], q_ref[rows, cols]
            score = (dot(g, v_ref[rows, cols], NT) * jnp.where(same, dec_ref[h], 0.0)).astype(BF16)
            carried = jnp.where(live, qdec_ref[h], 0.0) * dot(g, state_of(prev_ref, i, h), NT)
            qout_ref[rows, cols] = (dot(score, k, NN) + carried).astype(BF16)
            att_ref[rows, cols] = dot(score, q, TN)
            vgp_ref[rows, cols] = dot(mix_ref[i * heads + h], g, TN)
        return 0

    early = groups * 3 // 8
    lax.fori_loop(0, early, local_group, 0)
    sent(send2)
    turn(got2_ref, after_ref, 2, True, recv3, send4, recv4a, recv4b)
    lax.fori_loop(early, groups, local_group, 0)
    own_back(after_ref, 0, 3).wait()
    own_back(after_ref, 1, 3).wait()

    def final_group(i, _):
        rows = rows_of(i)
        live = segc_ref[i] == last_ref[i]
        for h in range(heads):
            cols = cols_of(h)
            after = state_of(after_ref, i, h)
            w = jnp.where(live, kdec_ref[h], 0.0)
            kout_ref[rows, cols] = (att_ref[rows, cols] + w * dot(v_ref[rows, cols], after, NT)).astype(BF16)
            vout_ref[rows, cols] = (vgp_ref[rows, cols] + w * dot(k_ref[rows, cols], after, NN)).astype(BF16)
        return 0

    def final_chunk(c, _):
        turned(after_ref, c, recv4a, recv4b)
        lax.fori_loop(c * CHUNK, (c + 1) * CHUNK, final_group, 0)
        return 0

    lax.fori_loop(0, chunks, final_chunk, 0)
    sent(send3)
    sent(send4)


def store_kernel(a_ref, b_ref, c_ref, ao_ref, bo_ref, co_ref, sem):
    pairs = ((a_ref, ao_ref), (b_ref, bo_ref), (c_ref, co_ref))
    copies = [pltpu.make_async_copy(src, dst, sem.at[n]) for n, (src, dst) in enumerate(pairs)]
    for copy in copies:
        copy.start()
    for copy in copies:
        copy.wait()


def shards(q, k, v, u, gain, rate, lengths, home):
    devices = lax.axis_size("seq")
    sides = lax.axis_size("head")
    heads = q.shape[1] // HEAD
    groups = home.shape[0]
    rows, width = q.shape
    docs = lengths.shape[0]
    total = devices * groups
    chunks = groups // CHUNK
    part = HEAD // RING // 2
    any_ = pl.BlockSpec(memory_space=pl.ANY)
    vmem, dma = pltpu.VMEM, pltpu.SemaphoreType.DMA
    table = vmem((heads, GROUP, GROUP), F32)
    strip = vmem((groups, 1, HEAD), F32)
    token = vmem((rows, width), BF16)
    flat = vmem((total, part, HEAD), BF16)
    state = vmem((2, devices, groups, part, HEAD), BF16)
    wide = vmem((rows, width), F32)
    scratch = (
        [pltpu.SMEM((heads,), F32), pltpu.SMEM((docs,), I32), pltpu.SMEM((groups,), I32)]
        + [vmem((1, width), F32), dma((4,))]
        + [token] * 4 + [state] + [flat] * 5 + [vmem((2, total, part, HEAD), BF16), state, state]
        + [wide, wide, vmem((groups * heads, GROUP, GROUP), BF16)]
        + [table] * 3 + [strip] * 3 + [vmem((groups, GROUP, GROUP), F32)]
        + [vmem((8, HEAD), I32), vmem((devices, 8, HEAD), I32), vmem((devices, HEAD), I32)]
        + [vmem((8, HEAD), I32), vmem((8, HEAD), F32)]
        + [pltpu.SMEM((devices, HEAD), I32), pltpu.SMEM((8, HEAD), I32), pltpu.SMEM((8, HEAD), F32)]
        + [vmem((chunks, 2 * CHUNK, HEAD), F32), vmem((chunks, sides - 1, 2 * CHUNK, HEAD), F32)]
        + [dma((2, chunks)), dma((2,)), dma((4, 2)), dma((3,)), dma, dma]
        + [dma, dma((2,)), dma, dma((2,)), dma((chunks,))] * 2
        + [dma((chunks,)), dma((chunks,))]
    )
    grads = pl.pallas_call(
        functools.partial(fused_kernel, heads, groups, devices, sides, docs),
        out_shape=(pltpu.VMEM((rows, width), BF16),) * 3,
        in_specs=[any_] * 8,
        out_specs=(pl.BlockSpec(memory_space=vmem),) * 3,
        scratch_shapes=scratch,
        compiler_params=pltpu.CompilerParams(
            collective_id=0, has_side_effects=True, vmem_limit_bytes=50 << 20
        ),
    )(rate, lengths, home, gain.reshape(1, width), q, k, v, u)
    return pl.pallas_call(
        store_kernel,
        out_shape=(jax.ShapeDtypeStruct((rows, width), BF16),) * 3,
        in_specs=[pl.BlockSpec(memory_space=vmem)] * 3,
        out_specs=(any_,) * 3,
        scratch_shapes=[dma((3,))],
        compiler_params=pltpu.CompilerParams(vmem_limit_bytes=4 << 20),
    )(*[pltpu.with_memory_space_constraint(g, vmem) for g in grads])


def solution(mesh):
    rows = P("seq", "head")
    return jax.shard_map(
        shards,
        mesh=mesh,
        in_specs=(rows, rows, rows, rows, P("head"), P("head"), P(), P("seq")),
        out_specs=(rows, rows, rows),
        check_vma=False,
    )
```

```python
import functools

import jax
import jax.numpy as jnp
from jax import lax
from jax.experimental import pallas as pl
from jax.experimental.pallas import tpu as pltpu
from jax.sharding import PartitionSpec as P

HEAD = 128
GROUP = 128
RING = 4
CHUNK = 4
UNROLL = 8
STEPS = 16
EPSILON = 1e-06
MESH = pl.DeviceIdType.MESH
F32 = jnp.float32
BF16 = jnp.bfloat16
I32 = jnp.int32
NN = ((1,), (0,))
NT = ((1,), (1,))
TN = ((0,), (0,))


def dot(a, b, dims):
    return lax.dot_general(a, b, (dims, ((), ())), preferred_element_type=F32)


def cols_of(h):
    return slice(h * HEAD, (h + 1) * HEAD)


def iota(shape, dim):
    return lax.broadcasted_iota(I32, shape, dim)


def torus_offsets(ring):
    offsets = [(dy, dz) for dy in range(ring) for dz in range(ring) if (dy, dz) != (0, 0)]
    return sorted(offsets, key=lambda o: min(o[0], ring - o[0]) + min(o[1], ring - o[1]))


def wait_bytes(ref, sem):
    pltpu.make_async_copy(ref, ref, sem).wait()


def fused_kernel(
    heads, groups, devices, sides, docs,
    rate_hbm, len_hbm, home_hbm, gain_hbm, q_hbm, k_hbm, v_hbm, u_hbm,
    qout_ref, kout_ref, vout_ref,
    rate_ref, len_ref, home_ref, gain_ref, arg_sem,
    q_ref, k_ref, v_ref, u_ref, send_ref, got1a_ref, got1b_ref, got2a_ref, got2b_ref, seq_ref, back_ref, prev_ref, after_ref,
    att_ref, vgp_ref, mix_ref,
    dec_ref, qdec_ref, kdec_ref, segr_ref, bef_ref, last_ref, segc_ref,
    hmine_ref, hall_ref, hcomp_ref, order_ref, carry_ref, homes_s, order_s, carry_s,
    mine_ref, gsum_ref,
    kv_sem, qu_sem, own_sem, smem_sem, hsend, hrecv, send1, recv1, send2, recv2a, recv2b,
    send3, recv3, send4, recv4a, recv4b, ssend, srecv,
):
    me = lax.axis_index("seq")
    side = lax.axis_index("head")
    y, z = me // RING, lax.rem(me, RING)
    peers = [lax.rem(y + dy, RING) * RING + lax.rem(z + dz, RING) for dy, dz in torus_offsets(RING)]
    mates = [lax.rem(side + n, sides) for n in range(1, sides)]
    got1_ref, got2_ref = (got1a_ref, got1b_ref), (got2a_ref, got2b_ref)
    others = devices - 1
    total = devices * groups
    chunks = groups // CHUNK
    slab = CHUNK * GROUP
    part = HEAD // RING // 2

    small = [
        pltpu.make_async_copy(src, dst, arg_sem.at[n])
        for n, (src, dst) in enumerate(
            [(rate_hbm, rate_ref), (len_hbm, len_ref), (home_hbm, home_ref), (gain_hbm, gain_ref)]
        )
    ]
    for copy in small:
        copy.start()
    barrier = pltpu.get_barrier_semaphore()
    for peer in peers:
        pl.semaphore_signal(barrier, inc=1, device_id=(peer, side), device_id_type=MESH)
    for mate in mates:
        pl.semaphore_signal(barrier, inc=1, device_id=(me, mate), device_id_type=MESH)

    def slab_copy(hbm, ref, c, sem):
        rows = pl.ds(c * slab, slab)
        return pltpu.make_async_copy(hbm.at[rows], ref.at[rows], sem)

    for c in range(chunks):
        slab_copy(k_hbm, k_ref, c, kv_sem.at[0, c]).start()
        slab_copy(v_hbm, v_ref, c, kv_sem.at[1, c]).start()
    load_q = pltpu.make_async_copy(q_hbm, q_ref, qu_sem.at[0])
    load_u = pltpu.make_async_copy(u_hbm, u_ref, qu_sem.at[1])

    for copy in small:
        copy.wait()
    row = iota((GROUP, GROUP), 0).astype(F32)
    for h in range(heads):
        kdec_ref[h] = jnp.exp(-rate_ref[h] * (GROUP - 1.0 - row))

    home_rows = jnp.zeros((groups, HEAD), I32)
    home_lanes = jnp.zeros((8, HEAD), I32)
    group_row = iota((groups, HEAD), 0)
    lane8 = iota((8, HEAD), 1)
    for i in range(groups):
        home_rows = jnp.where(group_row == i, home_ref[i], home_rows)
        home_lanes = jnp.where(lane8 == i, home_ref[i], home_lanes)
    hmine_ref[...] = home_lanes
    hall_ref[me] = home_lanes
    steps = iota((8, HEAD), 0) * HEAD + lane8
    pos = home_rows * GROUP + iota((groups, HEAD), 1)
    pos_b = home_rows * GROUP - 1
    step_b = steps * GROUP - 1
    seg = jnp.zeros_like(pos)
    seg_b = jnp.zeros_like(pos)
    step_seg_b = jnp.zeros_like(steps)
    step_seg_e = jnp.zeros_like(steps)
    end = jnp.int32(0)
    for n in range(docs):
        end = end + len_ref[n]
        seg += (pos >= end).astype(I32)
        seg_b += (pos_b >= end).astype(I32)
        step_seg_b += (step_b >= end).astype(I32)
        step_seg_e += (step_b + GROUP >= end).astype(I32)
    seg_b = jnp.where(home_rows == 0, -1, seg_b).astype(F32)
    seg = seg.astype(F32)
    for i in range(groups):
        segr_ref[i] = seg[i : i + 1]
        bef_ref[i] = seg_b[i : i + 1]
        last_ref[i] = jnp.broadcast_to(seg[i : i + 1, GROUP - 1 :], (1, HEAD))
    own_rate = rate_ref[me // RING]
    keep = jnp.exp(jnp.zeros((8, HEAD), F32) - own_rate * GROUP)
    joined = (step_seg_b == step_seg_e) | (steps == 0)
    carry_ref[...] = jnp.where(joined, keep, 0.0)
    carry_copy = pltpu.make_async_copy(carry_ref, carry_s, smem_sem.at[0])
    carry_copy.start()

    def rows_of(i):
        return pl.ds(pl.multiple_of(i * GROUP, GROUP), GROUP)

    def scatter(got_ref, half, c, send_sem, recv_sem):
        for peer in peers:
            pltpu.make_async_remote_copy(
                src_ref=send_ref.at[half, peer, pl.ds(c * CHUNK, CHUNK)],
                dst_ref=got_ref[half].at[pl.ds(me * groups + c * CHUNK, CHUNK)],
                send_sem=send_sem, recv_sem=recv_sem.at[half],
                device_id=(peer, side), device_id_type=MESH,
            ).start()

    def give_back(dst_ref, half, start, size, send_sem, recv_sem):
        for peer in peers:
            pltpu.make_async_remote_copy(
                src_ref=back_ref.at[half, pl.ds(peer * groups + start, size)],
                dst_ref=dst_ref.at[half, me, pl.ds(start, size)],
                send_sem=send_sem, recv_sem=recv_sem,
                device_id=(peer, side), device_id_type=MESH,
            ).start()

    def own_slice(got_ref, half, n):
        return pltpu.make_async_copy(
            send_ref.at[half, me], got_ref[half].at[pl.ds(me * groups, groups)], own_sem.at[n, half]
        )

    def own_back(dst_ref, half, n):
        return pltpu.make_async_copy(
            back_ref.at[half, pl.ds(me * groups, groups)], dst_ref.at[half, me], own_sem.at[n, half]
        )

    def store_state(i, h, s):
        send_ref[:, RING * h : RING * (h + 1), i] = s.astype(BF16).reshape(2, RING, part, HEAD)

    def state_of(ref, i, h):
        return ref[:, RING * h : RING * (h + 1), i].reshape(HEAD, HEAD)

    def summary_group(i, _):
        rows = rows_of(i)
        seg_c = jnp.broadcast_to(segr_ref[i], (GROUP, GROUP)).T
        segc_ref[i] = seg_c
        live = seg_c == last_ref[i]
        for h in range(heads):
            cols = cols_of(h)
            w = (jnp.where(live, kdec_ref[h], 0.0) * v_ref[rows, cols].astype(F32)).astype(BF16)
            store_state(i, h, dot(k_ref[rows, cols], w, TN))
        return 0

    def summarize(c):
        slab_copy(k_hbm, k_ref, c, kv_sem.at[0, c]).wait()
        slab_copy(v_hbm, v_ref, c, kv_sem.at[1, c]).wait()
        lax.fori_loop(c * CHUNK, (c + 1) * CHUNK, summary_group, 0)

    def summary_chunk(c, _):
        summarize(c)
        scatter(got1_ref, 0, c, send1, recv1)
        return 0

    summarize(0)
    load_q.start()
    load_u.start()
    pl.semaphore_wait(barrier, others + sides - 1)
    scatter(got1_ref, 0, 0, send1, recv1)
    for peer in peers:
        pltpu.make_async_remote_copy(
            src_ref=hmine_ref, dst_ref=hall_ref.at[me], send_sem=hsend, recv_sem=hrecv,
            device_id=(peer, side), device_id_type=MESH,
        ).start()
    lax.fori_loop(1, chunks, summary_chunk, 0)

    def second_half(c, _):
        scatter(got1_ref, 1, c, send1, recv1)
        return 0

    lax.fori_loop(0, chunks, second_half, 0)
    own_slice(got1_ref, 0, 0).start()
    own_slice(got1_ref, 1, 0).start()

    spread = row - iota((GROUP, GROUP), 1).astype(F32)
    for h in range(heads):
        r = rate_ref[h]
        dec_ref[h] = jnp.where(spread >= 0.0, jnp.exp(-r * jnp.maximum(spread, 0.0)), 0.0)
        qdec_ref[h] = jnp.exp(-r * (row + 1.0))

    wait_bytes(hall_ref.at[pl.ds(0, others)], hrecv)
    for d in range(devices):
        hcomp_ref[d : d + 1] = hall_ref[d, 0:1]
    homes_copy = pltpu.make_async_copy(hcomp_ref, homes_s, smem_sem.at[1])
    homes_copy.start()
    homes_copy.wait()

    def invert(b, acc):
        for n in range(UNROLL):
            p = b * UNROLL + n
            acc = jnp.where(steps == homes_s[p // groups, lax.rem(p, groups)], p, acc)
        return acc

    order_ref[...] = lax.fori_loop(0, total // UNROLL, invert, jnp.zeros((8, HEAD), I32))
    order_copy = pltpu.make_async_copy(order_ref, order_s, smem_sem.at[2])
    order_copy.start()
    load_q.wait()
    load_u.wait()

    def inner_group(i, _):
        rows = rows_of(i)
        same = segc_ref[i] == segr_ref[i]
        for h in range(heads):
            cols = cols_of(h)
            scores = dot(q_ref[rows, cols], k_ref[rows, cols], NT)
            mixing = (scores * jnp.where(same, dec_ref[h], 0.0)).astype(BF16)
            mix_ref[i * heads + h] = mixing
            att_ref[rows, cols] = dot(mixing, v_ref[rows, cols], NN)
        return 0

    lax.fori_loop(0, groups, inner_group, 0)
    order_copy.wait()
    carry_copy.wait()

    def scan(got_ref, half, reverse):
        def step(b, state):
            base = (total // STEPS - 1 - b if reverse else b) * STEPS
            hi, lo = base // HEAD, lax.rem(base, HEAD)
            arrived = [got_ref[half][order_s[hi, lo + n]] for n in range(STEPS)]
            keeps = [carry_s[hi, lo + n] for n in range(STEPS)]
            states = [None] * STEPS
            for n in range(STEPS):
                n = STEPS - 1 - n if reverse else n
                states[n] = state.astype(BF16)
                state = keeps[n] * state + arrived[n].astype(F32)
            for n in range(STEPS):
                seq_ref[base + n] = states[n]
            return state

        lax.fori_loop(0, total // STEPS, step, jnp.zeros((part, HEAD), F32))

        def put(d, _):
            found = [seq_ref[homes_s[d, n]] for n in range(groups)]
            for n in range(groups):
                back_ref[half, d * groups + n] = found[n]
            return 0

        lax.fori_loop(0, devices, put, 0)

    half_groups = groups // 2

    def turn(got_ref, dst_ref, n, reverse, recv_sem, send_back, recv_first, recv_second):
        own_slice(got_ref, 0, n).wait()
        wait_bytes(got_ref[0].at[pl.ds(0, others * groups)], recv_sem.at[0])
        scan(got_ref, 0, reverse)
        give_back(dst_ref, 0, 0, half_groups, send_back, recv_first.at[0])
        own_back(dst_ref, 0, n + 1).start()
        own_slice(got_ref, 1, n).wait()
        wait_bytes(got_ref[1].at[pl.ds(0, others * groups)], recv_sem.at[1])
        scan(got_ref, 1, reverse)
        own_back(dst_ref, 1, n + 1).start()

        def rest(c, _):
            @pl.when(c == chunks // 2)
            def _():
                give_back(dst_ref, 0, half_groups, half_groups, send_back, recv_first.at[1])

            give_back(dst_ref, 1, c * CHUNK, CHUNK, send_back, recv_second.at[c])
            return 0

        lax.fori_loop(0, chunks, rest, 0)

    def turned(dst_ref, c, recv_first, recv_second):
        @pl.when(lax.rem(c, chunks // 2) == 0)
        def _():
            wait_bytes(
                dst_ref.at[0, pl.ds(0, others), pl.ds(0, half_groups)], recv_first.at[c // (chunks // 2)]
            )

        wait_bytes(dst_ref.at[1, pl.ds(0, others), pl.ds(0, CHUNK)], recv_second.at[c])

    def sent(sem):
        wait_bytes(send_ref.at[0, pl.ds(0, others)], sem)
        wait_bytes(send_ref.at[0, pl.ds(0, others)], sem)

    turn(got1_ref, prev_ref, 0, False, recv1, send2, recv2a, recv2b)
    sent(send1)
    wait_bytes(hall_ref.at[pl.ds(0, others)], hsend)
    own_back(prev_ref, 0, 1).wait()
    own_back(prev_ref, 1, 1).wait()

    lane = iota((GROUP, HEAD), 1)
    pieces = GROUP // (2 * CHUNK)
    width = 2 * CHUNK

    def output_group(c, g, acc):
        i = c * CHUNK + g
        rows = rows_of(i)
        live = segc_ref[i] == bef_ref[i]
        squares = jnp.zeros((GROUP, HEAD), F32)
        crossed = jnp.zeros((GROUP, HEAD), F32)
        for h in range(heads):
            cols = cols_of(h)
            carried = dot(q_ref[rows, cols], state_of(prev_ref, i, h), NN)
            out = att_ref[rows, cols] + jnp.where(live, qdec_ref[h], 0.0) * carried
            att_ref[rows, cols] = out
            squares += out * out
            crossed += gain_ref[:, cols] * u_ref[rows, cols].astype(F32) * out
        squares = jnp.sum(squares, axis=1, keepdims=True)
        crossed = jnp.sum(crossed, axis=1, keepdims=True)
        return jnp.where(lane == g, squares, jnp.where(lane == g + CHUNK, crossed, acc))

    def total_copy(c, n):
        return pltpu.make_async_remote_copy(
            src_ref=mine_ref.at[c], dst_ref=gsum_ref.at[c, n], send_sem=ssend.at[c], recv_sem=srecv.at[c],
            device_id=(me, mates[n]), device_id_type=MESH,
        )

    def output_chunk(c):
        turned(prev_ref, c, recv2a, recv2b)
        acc = lax.fori_loop(0, CHUNK, functools.partial(output_group, c), jnp.zeros((GROUP, HEAD), F32))
        packed = acc[0:width]
        for n in range(1, pieces):
            packed += pltpu.roll(acc[n * width : (n + 1) * width], n * width, 1)
        mine_ref[c] = packed
        for n in range(sides - 1):
            total_copy(c, n).start()

    channels = heads * HEAD * sides

    def cotangent_group(c, sums, g, _):
        i = c * CHUNK + g
        rows = rows_of(i)
        live = segc_ref[i] == bef_ref[i]
        squares = jnp.sum(jnp.where(lane == g, sums, 0.0), axis=1, keepdims=True)
        crossed = jnp.sum(jnp.where(lane == g + CHUNK, sums, 0.0), axis=1, keepdims=True)
        scaling = lax.rsqrt(squares / channels + EPSILON)
        pull = scaling * scaling * scaling * (crossed / channels)
        for h in range(heads):
            cols = cols_of(h)
            wide = gain_ref[:, cols] * u_ref[rows, cols].astype(F32)
            grad = (scaling * wide - pull * att_ref[rows, cols]).astype(BF16)
            u_ref[rows, cols] = grad
            w = (jnp.where(live, qdec_ref[h], 0.0) * grad.astype(F32)).astype(BF16)
            store_state(i, h, dot(q_ref[rows, cols], w, TN))
        return 0

    def cotangent_chunk(c):
        wait_bytes(gsum_ref.at[c], srecv.at[c])
        wait_bytes(gsum_ref.at[c], ssend.at[c])
        both = mine_ref[c]
        for n in range(sides - 1):
            both += gsum_ref[c, n]
        sums = jnp.concatenate(
            [both] + [pltpu.roll(both, HEAD - n * width, 1) for n in range(1, pieces)], axis=0
        )
        lax.fori_loop(0, CHUNK, functools.partial(cotangent_group, c, sums), 0)
        scatter(got2_ref, 0, c, send3, recv3)

        @pl.when(c < chunks - 2)
        def _():
            scatter(got2_ref, 1, c, send3, recv3)

    def middle(c, _):
        @pl.when(c < chunks)
        def _():
            output_chunk(c)

        @pl.when(c >= 1)
        def _():
            cotangent_chunk(c - 1)

        return 0

    lax.fori_loop(0, chunks + 1, middle, 0)
    for c in (chunks - 2, chunks - 1):
        scatter(got2_ref, 1, c, send3, recv3)
    own_slice(got2_ref, 0, 2).start()
    own_slice(got2_ref, 1, 2).start()

    def local_group(i, _):
        rows = rows_of(i)
        seg_c = segc_ref[i]
        same = seg_c == segr_ref[i]
        live = seg_c == bef_ref[i]
        for h in range(heads):
            cols = cols_of(h)
            g, k, q = u_ref[rows, cols], k_ref[rows, cols], q_ref[rows, cols]
            score = (dot(g, v_ref[rows, cols], NT) * jnp.where(same, dec_ref[h], 0.0)).astype(BF16)
            carried = jnp.where(live, qdec_ref[h], 0.0) * dot(g, state_of(prev_ref, i, h), NT)
            qout_ref[rows, cols] = (dot(score, k, NN) + carried).astype(BF16)
            att_ref[rows, cols] = dot(score, q, TN)
            vgp_ref[rows, cols] = dot(mix_ref[i * heads + h], g, TN)
        return 0

    early = groups * 3 // 8
    lax.fori_loop(0, early, local_group, 0)
    sent(send2)
    turn(got2_ref, after_ref, 2, True, recv3, send4, recv4a, recv4b)
    lax.fori_loop(early, groups, local_group, 0)
    own_back(after_ref, 0, 3).wait()
    own_back(after_ref, 1, 3).wait()

    def final_group(i, _):
        rows = rows_of(i)
        live = segc_ref[i] == last_ref[i]
        for h in range(heads):
            cols = cols_of(h)
            after = state_of(after_ref, i, h)
            w = jnp.where(live, kdec_ref[h], 0.0)
            kout_ref[rows, cols] = (att_ref[rows, cols] + w * dot(v_ref[rows, cols], after, NT)).astype(BF16)
            vout_ref[rows, cols] = (vgp_ref[rows, cols] + w * dot(k_ref[rows, cols], after, NN)).astype(BF16)
        return 0

    def final_chunk(c, _):
        turned(after_ref, c, recv4a, recv4b)
        lax.fori_loop(c * CHUNK, (c + 1) * CHUNK, final_group, 0)
        return 0

    lax.fori_loop(0, chunks, final_chunk, 0)
    sent(send3)
    sent(send4)


def store_kernel(a_ref, b_ref, c_ref, ao_ref, bo_ref, co_ref, sem):
    pairs = ((a_ref, ao_ref), (b_ref, bo_ref), (c_ref, co_ref))
    copies = [pltpu.make_async_copy(src, dst, sem.at[n]) for n, (src, dst) in enumerate(pairs)]
    for copy in copies:
        copy.start()
    for copy in copies:
        copy.wait()


def shards(q, k, v, u, gain, rate, lengths, home):
    devices = lax.axis_size("seq")
    sides = lax.axis_size("head")
    heads = q.shape[1] // HEAD
    groups = home.shape[0]
    rows, width = q.shape
    docs = lengths.shape[0]
    total = devices * groups
    chunks = groups // CHUNK
    part = HEAD // RING // 2
    any_ = pl.BlockSpec(memory_space=pl.ANY)
    vmem, dma = pltpu.VMEM, pltpu.SemaphoreType.DMA
    table = vmem((heads, GROUP, GROUP), F32)
    strip = vmem((groups, 1, HEAD), F32)
    token = vmem((rows, width), BF16)
    flat = vmem((total, part, HEAD), BF16)
    state = vmem((2, devices, groups, part, HEAD), BF16)
    wide = vmem((rows, width), F32)
    scratch = (
        [pltpu.SMEM((heads,), F32), pltpu.SMEM((docs,), I32), pltpu.SMEM((groups,), I32)]
        + [vmem((1, width), F32), dma((4,))]
        + [token] * 4 + [state] + [flat] * 5 + [vmem((2, total, part, HEAD), BF16), state, state]
        + [wide, wide, vmem((groups * heads, GROUP, GROUP), BF16)]
        + [table] * 3 + [strip] * 3 + [vmem((groups, GROUP, GROUP), F32)]
        + [vmem((8, HEAD), I32), vmem((devices, 8, HEAD), I32), vmem((devices, HEAD), I32)]
        + [vmem((8, HEAD), I32), vmem((8, HEAD), F32)]
        + [pltpu.SMEM((devices, HEAD), I32), pltpu.SMEM((8, HEAD), I32), pltpu.SMEM((8, HEAD), F32)]
        + [vmem((chunks, 2 * CHUNK, HEAD), F32), vmem((chunks, sides - 1, 2 * CHUNK, HEAD), F32)]
        + [dma((2, chunks)), dma((2,)), dma((4, 2)), dma((3,)), dma, dma]
        + [dma, dma((2,)), dma, dma((2,)), dma((chunks,))] * 2
        + [dma((chunks,)), dma((chunks,))]
    )
    grads = pl.pallas_call(
        functools.partial(fused_kernel, heads, groups, devices, sides, docs),
        out_shape=(pltpu.VMEM((rows, width), BF16),) * 3,
        in_specs=[any_] * 8,
        out_specs=(pl.BlockSpec(memory_space=vmem),) * 3,
        scratch_shapes=scratch,
        compiler_params=pltpu.CompilerParams(
            collective_id=0, has_side_effects=True, vmem_limit_bytes=50 << 20
        ),
    )(rate, lengths, home, gain.reshape(1, width), q, k, v, u)
    return pl.pallas_call(
        store_kernel,
        out_shape=(jax.ShapeDtypeStruct((rows, width), BF16),) * 3,
        in_specs=[pl.BlockSpec(memory_space=vmem)] * 3,
        out_specs=(any_,) * 3,
        scratch_shapes=[dma((3,))],
        compiler_params=pltpu.CompilerParams(vmem_limit_bytes=4 << 20),
    )(*[pltpu.with_memory_space_constraint(g, vmem) for g in grads])


def solution(mesh):
    rows = P("seq", "head")
    return jax.shard_map(
        shards,
        mesh=mesh,
        in_specs=(rows, rows, rows, rows, P("head"), P("head"), P(), P("seq")),
        out_specs=(rows, rows, rows),
        check_vma=False,
    )
```

```python
import functools

import jax
import jax.numpy as jnp
from jax import lax
from jax.experimental import pallas as pl
from jax.experimental.pallas import tpu as pltpu
from jax.sharding import PartitionSpec as P

HEAD = 128
GROUP = 128
RING = 4
CHUNK = 4
UNROLL = 8
STEPS = 16
EPSILON = 1e-06
MESH = pl.DeviceIdType.MESH
F32 = jnp.float32
BF16 = jnp.bfloat16
I32 = jnp.int32
NN = ((1,), (0,))
NT = ((1,), (1,))
TN = ((0,), (0,))


def dot(a, b, dims):
    return lax.dot_general(a, b, (dims, ((), ())), preferred_element_type=F32)


def cols_of(h):
    return slice(h * HEAD, (h + 1) * HEAD)


def iota(shape, dim):
    return lax.broadcasted_iota(I32, shape, dim)


def torus_offsets(ring):
    offsets = [(dy, dz) for dy in range(ring) for dz in range(ring) if (dy, dz) != (0, 0)]
    return sorted(offsets, key=lambda o: min(o[0], ring - o[0]) + min(o[1], ring - o[1]))


def wait_bytes(ref, sem):
    pltpu.make_async_copy(ref, ref, sem).wait()


def fused_kernel(
    heads, groups, devices, sides, docs,
    rate_hbm, len_hbm, home_hbm, gain_hbm, q_hbm, k_hbm, v_hbm, u_hbm,
    qout_ref, kout_ref, vout_ref,
    rate_ref, len_ref, home_ref, gain_ref, arg_sem,
    q_ref, k_ref, v_ref, u_ref, send_ref, got1a_ref, got1b_ref, got2a_ref, got2b_ref, seq_ref, back_ref, prev_ref, after_ref,
    att_ref, vgp_ref, mix_ref,
    dec_ref, qdec_ref, kdec_ref, segr_ref, bef_ref, last_ref, segc_ref,
    hmine_ref, hall_ref, hcomp_ref, order_ref, carry_ref, homes_s, order_s, carry_s,
    mine_ref, gsum_ref,
    kv_sem, qu_sem, own_sem, smem_sem, hsend, hrecv, send1, recv1, send2, recv2a, recv2b,
    send3, recv3, send4, recv4a, recv4b, ssend, srecv,
):
    me = lax.axis_index("seq")
    side = lax.axis_index("head")
    y, z = me // RING, lax.rem(me, RING)
    peers = [lax.rem(y + dy, RING) * RING + lax.rem(z + dz, RING) for dy, dz in torus_offsets(RING)]
    mates = [lax.rem(side + n, sides) for n in range(1, sides)]
    got1_ref, got2_ref = (got1a_ref, got1b_ref), (got2a_ref, got2b_ref)
    others = devices - 1
    total = devices * groups
    chunks = groups // CHUNK
    slab = CHUNK * GROUP
    part = HEAD // RING // 2

    small = [
        pltpu.make_async_copy(src, dst, arg_sem.at[n])
        for n, (src, dst) in enumerate(
            [(rate_hbm, rate_ref), (len_hbm, len_ref), (home_hbm, home_ref), (gain_hbm, gain_ref)]
        )
    ]
    for copy in small:
        copy.start()
    barrier = pltpu.get_barrier_semaphore()
    for peer in peers:
        pl.semaphore_signal(barrier, inc=1, device_id=(peer, side), device_id_type=MESH)
    for mate in mates:
        pl.semaphore_signal(barrier, inc=1, device_id=(me, mate), device_id_type=MESH)

    def slab_copy(hbm, ref, c, sem):
        rows = pl.ds(c * slab, slab)
        return pltpu.make_async_copy(hbm.at[rows], ref.at[rows], sem)

    for c in range(chunks):
        slab_copy(k_hbm, k_ref, c, kv_sem.at[0, c]).start()
        slab_copy(v_hbm, v_ref, c, kv_sem.at[1, c]).start()
    load_q = pltpu.make_async_copy(q_hbm, q_ref, qu_sem.at[0])
    load_u = pltpu.make_async_copy(u_hbm, u_ref, qu_sem.at[1])

    for copy in small:
        copy.wait()
    row = iota((GROUP, GROUP), 0).astype(F32)
    for h in range(heads):
        kdec_ref[h] = jnp.exp(-rate_ref[h] * (GROUP - 1.0 - row))

    home_rows = jnp.zeros((groups, HEAD), I32)
    home_lanes = jnp.zeros((8, HEAD), I32)
    group_row = iota((groups, HEAD), 0)
    lane8 = iota((8, HEAD), 1)
    for i in range(groups):
        home_rows = jnp.where(group_row == i, home_ref[i], home_rows)
        home_lanes = jnp.where(lane8 == i, home_ref[i], home_lanes)
    hmine_ref[...] = home_lanes
    hall_ref[me] = home_lanes
    steps = iota((8, HEAD), 0) * HEAD + lane8
    pos = home_rows * GROUP + iota((groups, HEAD), 1)
    pos_b = home_rows * GROUP - 1
    step_b = steps * GROUP - 1
    seg = jnp.zeros_like(pos)
    seg_b = jnp.zeros_like(pos)
    step_seg_b = jnp.zeros_like(steps)
    step_seg_e = jnp.zeros_like(steps)
    end = jnp.int32(0)
    for n in range(docs):
        end = end + len_ref[n]
        seg += (pos >= end).astype(I32)
        seg_b += (pos_b >= end).astype(I32)
        step_seg_b += (step_b >= end).astype(I32)
        step_seg_e += (step_b + GROUP >= end).astype(I32)
    seg_b = jnp.where(home_rows == 0, -1, seg_b).astype(F32)
    seg = seg.astype(F32)
    for i in range(groups):
        segr_ref[i] = seg[i : i + 1]
        bef_ref[i] = seg_b[i : i + 1]
        last_ref[i] = jnp.broadcast_to(seg[i : i + 1, GROUP - 1 :], (1, HEAD))
    own_rate = rate_ref[me // RING]
    keep = jnp.exp(jnp.zeros((8, HEAD), F32) - own_rate * GROUP)
    joined = (step_seg_b == step_seg_e) | (steps == 0)
    carry_ref[...] = jnp.where(joined, keep, 0.0)
    carry_copy = pltpu.make_async_copy(carry_ref, carry_s, smem_sem.at[0])
    carry_copy.start()

    def rows_of(i):
        return pl.ds(pl.multiple_of(i * GROUP, GROUP), GROUP)

    def scatter(got_ref, half, c, send_sem, recv_sem):
        for peer in peers:
            pltpu.make_async_remote_copy(
                src_ref=send_ref.at[half, peer, pl.ds(c * CHUNK, CHUNK)],
                dst_ref=got_ref[half].at[pl.ds(me * groups + c * CHUNK, CHUNK)],
                send_sem=send_sem, recv_sem=recv_sem.at[half],
                device_id=(peer, side), device_id_type=MESH,
            ).start()

    def give_back(dst_ref, half, start, size, send_sem, recv_sem):
        for peer in peers:
            pltpu.make_async_remote_copy(
                src_ref=back_ref.at[half, pl.ds(peer * groups + start, size)],
                dst_ref=dst_ref.at[half, me, pl.ds(start, size)],
                send_sem=send_sem, recv_sem=recv_sem,
                device_id=(peer, side), device_id_type=MESH,
            ).start()

    def own_slice(got_ref, half, n):
        return pltpu.make_async_copy(
            send_ref.at[half, me], got_ref[half].at[pl.ds(me * groups, groups)], own_sem.at[n, half]
        )

    def own_back(dst_ref, half, n):
        return pltpu.make_async_copy(
            back_ref.at[half, pl.ds(me * groups, groups)], dst_ref.at[half, me], own_sem.at[n, half]
        )

    def store_state(i, h, s):
        send_ref[:, RING * h : RING * (h + 1), i] = s.astype(BF16).reshape(2, RING, part, HEAD)

    def state_of(ref, i, h):
        return ref[:, RING * h : RING * (h + 1), i].reshape(HEAD, HEAD)

    def summary_group(i, _):
        rows = rows_of(i)
        seg_c = jnp.broadcast_to(segr_ref[i], (GROUP, GROUP)).T
        segc_ref[i] = seg_c
        live = seg_c == last_ref[i]
        for h in range(heads):
            cols = cols_of(h)
            w = (jnp.where(live, kdec_ref[h], 0.0) * v_ref[rows, cols].astype(F32)).astype(BF16)
            store_state(i, h, dot(k_ref[rows, cols], w, TN))
        return 0

    def summarize(c):
        slab_copy(k_hbm, k_ref, c, kv_sem.at[0, c]).wait()
        slab_copy(v_hbm, v_ref, c, kv_sem.at[1, c]).wait()
        lax.fori_loop(c * CHUNK, (c + 1) * CHUNK, summary_group, 0)

    def summary_chunk(c, _):
        summarize(c)
        scatter(got1_ref, 0, c, send1, recv1)
        return 0

    slab_copy(k_hbm, k_ref, 0, kv_sem.at[0, 0]).wait()
    slab_copy(v_hbm, v_ref, 0, kv_sem.at[1, 0]).wait()
    first = CHUNK // 2
    lax.fori_loop(0, first, summary_group, 0)
    pl.semaphore_wait(barrier, others + sides - 1)

    def first_piece(n, _):
        for peer in peers:
            pltpu.make_async_remote_copy(
                src_ref=send_ref.at[0, peer, pl.ds(n * first, first)],
                dst_ref=got1_ref[0].at[pl.ds(me * groups + n * first, first)],
                send_sem=send1, recv_sem=recv1.at[0],
                device_id=(peer, side), device_id_type=MESH,
            ).start()
        lax.fori_loop((n + 1) * first, (n + 2) * first * (1 - n), summary_group, 0)
        return 0

    lax.fori_loop(0, 2, first_piece, 0)
    load_q.start()
    load_u.start()
    for peer in peers:
        pltpu.make_async_remote_copy(
            src_ref=hmine_ref, dst_ref=hall_ref.at[me], send_sem=hsend, recv_sem=hrecv,
            device_id=(peer, side), device_id_type=MESH,
        ).start()
    lax.fori_loop(1, chunks, summary_chunk, 0)

    def second_half(c, _):
        scatter(got1_ref, 1, c, send1, recv1)
        return 0

    lax.fori_loop(0, chunks, second_half, 0)
    own_slice(got1_ref, 0, 0).start()
    own_slice(got1_ref, 1, 0).start()

    spread = row - iota((GROUP, GROUP), 1).astype(F32)
    for h in range(heads):
        r = rate_ref[h]
        dec_ref[h] = jnp.where(spread >= 0.0, jnp.exp(-r * jnp.maximum(spread, 0.0)), 0.0)
        qdec_ref[h] = jnp.exp(-r * (row + 1.0))

    wait_bytes(hall_ref.at[pl.ds(0, others)], hrecv)
    for d in range(devices):
        hcomp_ref[d : d + 1] = hall_ref[d, 0:1]
    homes_copy = pltpu.make_async_copy(hcomp_ref, homes_s, smem_sem.at[1])
    homes_copy.start()
    homes_copy.wait()

    def invert(b, acc):
        for n in range(UNROLL):
            p = b * UNROLL + n
            acc = jnp.where(steps == homes_s[p // groups, lax.rem(p, groups)], p, acc)
        return acc

    order_ref[...] = lax.fori_loop(0, total // UNROLL, invert, jnp.zeros((8, HEAD), I32))
    order_copy = pltpu.make_async_copy(order_ref, order_s, smem_sem.at[2])
    order_copy.start()
    load_q.wait()
    load_u.wait()

    def inner_group(i, _):
        rows = rows_of(i)
        same = segc_ref[i] == segr_ref[i]
        for h in range(heads):
            cols = cols_of(h)
            scores = dot(q_ref[rows, cols], k_ref[rows, cols], NT)
            mixing = (scores * jnp.where(same, dec_ref[h], 0.0)).astype(BF16)
            mix_ref[i * heads + h] = mixing
            att_ref[rows, cols] = dot(mixing, v_ref[rows, cols], NN)
        return 0

    lax.fori_loop(0, groups, inner_group, 0)
    order_copy.wait()
    carry_copy.wait()

    def scan(got_ref, half, reverse):
        def step(b, state):
            base = (total // STEPS - 1 - b if reverse else b) * STEPS
            hi, lo = base // HEAD, lax.rem(base, HEAD)
            arrived = [got_ref[half][order_s[hi, lo + n]] for n in range(STEPS)]
            keeps = [carry_s[hi, lo + n] for n in range(STEPS)]
            states = [None] * STEPS
            for n in range(STEPS):
                n = STEPS - 1 - n if reverse else n
                states[n] = state.astype(BF16)
                state = keeps[n] * state + arrived[n].astype(F32)
            for n in range(STEPS):
                seq_ref[base + n] = states[n]
            return state

        lax.fori_loop(0, total // STEPS, step, jnp.zeros((part, HEAD), F32))

        def put(d, _):
            found = [seq_ref[homes_s[d, n]] for n in range(groups)]
            for n in range(groups):
                back_ref[half, d * groups + n] = found[n]
            return 0

        lax.fori_loop(0, devices, put, 0)

    half_groups = groups // 2
    piece = CHUNK // 2

    def turn(got_ref, dst_ref, n, reverse, recv_sem, send_back, recv_first, recv_second):
        own_slice(got_ref, 0, n).wait()
        wait_bytes(got_ref[0].at[pl.ds(0, others * groups)], recv_sem.at[0])
        scan(got_ref, 0, reverse)
        give_back(dst_ref, 0, 0, half_groups, send_back, recv_first.at[0])
        own_back(dst_ref, 0, n + 1).start()
        own_slice(got_ref, 1, n).wait()
        wait_bytes(got_ref[1].at[pl.ds(0, others * groups)], recv_sem.at[1])
        scan(got_ref, 1, reverse)
        own_back(dst_ref, 1, n + 1).start()

        def rest(c, _):
            @pl.when(c == chunks // 2)
            def _():
                give_back(dst_ref, 0, half_groups, half_groups, send_back, recv_first.at[1])

            give_back(dst_ref, 1, c * CHUNK, CHUNK, send_back, recv_second.at[c])
            return 0

        lax.fori_loop(0, chunks - 1, rest, 0)
        for n in range(2):
            give_back(dst_ref, 1, groups - CHUNK + n * piece, piece, send_back, recv_second.at[chunks - 1 + n])

    def turned(dst_ref, c, recv_first, recv_second):
        @pl.when(lax.rem(c, chunks // 2) == 0)
        def _():
            wait_bytes(
                dst_ref.at[0, pl.ds(0, others), pl.ds(0, half_groups)], recv_first.at[c // (chunks // 2)]
            )

        @pl.when(c < chunks - 1)
        def _():
            wait_bytes(dst_ref.at[1, pl.ds(0, others), pl.ds(0, CHUNK)], recv_second.at[c])

    def turned_piece(dst_ref, n, recv_second):
        wait_bytes(dst_ref.at[1, pl.ds(0, others), pl.ds(0, piece)], recv_second.at[chunks - 1 + n])

    def sent(sem):
        wait_bytes(send_ref.at[0, pl.ds(0, others)], sem)
        wait_bytes(send_ref.at[0, pl.ds(0, others)], sem)

    turn(got1_ref, prev_ref, 0, False, recv1, send2, recv2a, recv2b)
    sent(send1)
    wait_bytes(hall_ref.at[pl.ds(0, others)], hsend)
    own_back(prev_ref, 0, 1).wait()
    own_back(prev_ref, 1, 1).wait()

    lane = iota((GROUP, HEAD), 1)
    pieces = GROUP // (2 * CHUNK)
    width = 2 * CHUNK

    def output_group(c, g, acc):
        i = c * CHUNK + g
        rows = rows_of(i)
        live = segc_ref[i] == bef_ref[i]
        squares = jnp.zeros((GROUP, HEAD), F32)
        crossed = jnp.zeros((GROUP, HEAD), F32)
        for h in range(heads):
            cols = cols_of(h)
            carried = dot(q_ref[rows, cols], state_of(prev_ref, i, h), NN)
            out = att_ref[rows, cols] + jnp.where(live, qdec_ref[h], 0.0) * carried
            att_ref[rows, cols] = out
            squares += out * out
            crossed += gain_ref[:, cols] * u_ref[rows, cols].astype(F32) * out
        squares = jnp.sum(squares, axis=1, keepdims=True)
        crossed = jnp.sum(crossed, axis=1, keepdims=True)
        return jnp.where(lane == g, squares, jnp.where(lane == g + CHUNK, crossed, acc))

    def total_copy(c, n):
        return pltpu.make_async_remote_copy(
            src_ref=mine_ref.at[c], dst_ref=gsum_ref.at[c, n], send_sem=ssend.at[c], recv_sem=srecv.at[c],
            device_id=(me, mates[n]), device_id_type=MESH,
        )

    def output_chunk(c):
        turned(prev_ref, c, recv2a, recv2b)

        @pl.when(c == chunks - 1)
        def _():
            turned_piece(prev_ref, 0, recv2b)
            turned_piece(prev_ref, 1, recv2b)

        acc = lax.fori_loop(0, CHUNK, functools.partial(output_group, c), jnp.zeros((GROUP, HEAD), F32))
        packed = acc[0:width]
        for n in range(1, pieces):
            packed += pltpu.roll(acc[n * width : (n + 1) * width], n * width, 1)
        mine_ref[c] = packed
        for n in range(sides - 1):
            total_copy(c, n).start()

    channels = heads * HEAD * sides

    def cotangent_group(c, sums, g, _):
        i = c * CHUNK + g
        rows = rows_of(i)
        live = segc_ref[i] == bef_ref[i]
        squares = jnp.sum(jnp.where(lane == g, sums, 0.0), axis=1, keepdims=True)
        crossed = jnp.sum(jnp.where(lane == g + CHUNK, sums, 0.0), axis=1, keepdims=True)
        scaling = lax.rsqrt(squares / channels + EPSILON)
        pull = scaling * scaling * scaling * (crossed / channels)
        for h in range(heads):
            cols = cols_of(h)
            wide = gain_ref[:, cols] * u_ref[rows, cols].astype(F32)
            grad = (scaling * wide - pull * att_ref[rows, cols]).astype(BF16)
            u_ref[rows, cols] = grad
            w = (jnp.where(live, qdec_ref[h], 0.0) * grad.astype(F32)).astype(BF16)
            store_state(i, h, dot(q_ref[rows, cols], w, TN))
        return 0

    def cotangent_chunk(c):
        wait_bytes(gsum_ref.at[c], srecv.at[c])
        wait_bytes(gsum_ref.at[c], ssend.at[c])
        both = mine_ref[c]
        for n in range(sides - 1):
            both += gsum_ref[c, n]
        sums = jnp.concatenate(
            [both] + [pltpu.roll(both, HEAD - n * width, 1) for n in range(1, pieces)], axis=0
        )
        lax.fori_loop(0, CHUNK, functools.partial(cotangent_group, c, sums), 0)
        scatter(got2_ref, 0, c, send3, recv3)

        @pl.when(c < chunks - 2)
        def _():
            scatter(got2_ref, 1, c, send3, recv3)

    def middle(c, _):
        @pl.when(c < chunks)
        def _():
            output_chunk(c)

        @pl.when(c >= 1)
        def _():
            cotangent_chunk(c - 1)

        return 0

    lax.fori_loop(0, chunks + 1, middle, 0)
    for c in (chunks - 2, chunks - 1):
        scatter(got2_ref, 1, c, send3, recv3)
    own_slice(got2_ref, 0, 2).start()
    own_slice(got2_ref, 1, 2).start()

    def local_group(i, _):
        rows = rows_of(i)
        seg_c = segc_ref[i]
        same = seg_c == segr_ref[i]
        live = seg_c == bef_ref[i]
        for h in range(heads):
            cols = cols_of(h)
            g, k, q = u_ref[rows, cols], k_ref[rows, cols], q_ref[rows, cols]
            score = (dot(g, v_ref[rows, cols], NT) * jnp.where(same, dec_ref[h], 0.0)).astype(BF16)
            carried = jnp.where(live, qdec_ref[h], 0.0) * dot(g, state_of(prev_ref, i, h), NT)
            qout_ref[rows, cols] = (dot(score, k, NN) + carried).astype(BF16)
            att_ref[rows, cols] = dot(score, q, TN)
            vgp_ref[rows, cols] = dot(mix_ref[i * heads + h], g, TN)
        return 0

    early = groups * 3 // 8
    lax.fori_loop(0, early, local_group, 0)
    sent(send2)
    turn(got2_ref, after_ref, 2, True, recv3, send4, recv4a, recv4b)
    lax.fori_loop(early, groups, local_group, 0)
    own_back(after_ref, 0, 3).wait()
    own_back(after_ref, 1, 3).wait()

    def final_group(i, _):
        rows = rows_of(i)
        live = segc_ref[i] == last_ref[i]
        for h in range(heads):
            cols = cols_of(h)
            after = state_of(after_ref, i, h)
            w = jnp.where(live, kdec_ref[h], 0.0)
            kout_ref[rows, cols] = (att_ref[rows, cols] + w * dot(v_ref[rows, cols], after, NT)).astype(BF16)
            vout_ref[rows, cols] = (vgp_ref[rows, cols] + w * dot(k_ref[rows, cols], after, NN)).astype(BF16)
        return 0

    def final_chunk(c, _):
        turned(after_ref, c, recv4a, recv4b)
        lax.fori_loop(c * CHUNK, (c + 1) * CHUNK, final_group, 0)
        return 0

    lax.fori_loop(0, chunks - 1, final_chunk, 0)
    for n in range(2):
        turned_piece(after_ref, n, recv4b)
        start = groups - CHUNK + n * piece
        lax.fori_loop(start, start + piece, final_group, 0)
    sent(send3)
    sent(send4)


def store_kernel(a_ref, b_ref, c_ref, ao_ref, bo_ref, co_ref, sem):
    pairs = ((a_ref, ao_ref), (b_ref, bo_ref), (c_ref, co_ref))
    copies = [pltpu.make_async_copy(src, dst, sem.at[n]) for n, (src, dst) in enumerate(pairs)]
    for copy in copies:
        copy.start()
    for copy in copies:
        copy.wait()


def shards(q, k, v, u, gain, rate, lengths, home):
    devices = lax.axis_size("seq")
    sides = lax.axis_size("head")
    heads = q.shape[1] // HEAD
    groups = home.shape[0]
    rows, width = q.shape
    docs = lengths.shape[0]
    total = devices * groups
    chunks = groups // CHUNK
    part = HEAD // RING // 2
    any_ = pl.BlockSpec(memory_space=pl.ANY)
    vmem, dma = pltpu.VMEM, pltpu.SemaphoreType.DMA
    table = vmem((heads, GROUP, GROUP), F32)
    strip = vmem((groups, 1, HEAD), F32)
    token = vmem((rows, width), BF16)
    flat = vmem((total, part, HEAD), BF16)
    state = vmem((2, devices, groups, part, HEAD), BF16)
    wide = vmem((rows, width), F32)
    scratch = (
        [pltpu.SMEM((heads,), F32), pltpu.SMEM((docs,), I32), pltpu.SMEM((groups,), I32)]
        + [vmem((1, width), F32), dma((4,))]
        + [token] * 4 + [state] + [flat] * 5 + [vmem((2, total, part, HEAD), BF16), state, state]
        + [wide, wide, vmem((groups * heads, GROUP, GROUP), BF16)]
        + [table] * 3 + [strip] * 3 + [vmem((groups, GROUP, GROUP), F32)]
        + [vmem((8, HEAD), I32), vmem((devices, 8, HEAD), I32), vmem((devices, HEAD), I32)]
        + [vmem((8, HEAD), I32), vmem((8, HEAD), F32)]
        + [pltpu.SMEM((devices, HEAD), I32), pltpu.SMEM((8, HEAD), I32), pltpu.SMEM((8, HEAD), F32)]
        + [vmem((chunks, 2 * CHUNK, HEAD), F32), vmem((chunks, sides - 1, 2 * CHUNK, HEAD), F32)]
        + [dma((2, chunks)), dma((2,)), dma((4, 2)), dma((3,)), dma, dma]
        + [dma, dma((2,)), dma, dma((2,)), dma((chunks + 1,))] * 2
        + [dma((chunks,)), dma((chunks,))]
    )
    grads = pl.pallas_call(
        functools.partial(fused_kernel, heads, groups, devices, sides, docs),
        out_shape=(pltpu.VMEM((rows, width), BF16),) * 3,
        in_specs=[any_] * 8,
        out_specs=(pl.BlockSpec(memory_space=vmem),) * 3,
        scratch_shapes=scratch,
        compiler_params=pltpu.CompilerParams(
            collective_id=0, has_side_effects=True, vmem_limit_bytes=50 << 20
        ),
    )(rate, lengths, home, gain.reshape(1, width), q, k, v, u)
    return pl.pallas_call(
        store_kernel,
        out_shape=(jax.ShapeDtypeStruct((rows, width), BF16),) * 3,
        in_specs=[pl.BlockSpec(memory_space=vmem)] * 3,
        out_specs=(any_,) * 3,
        scratch_shapes=[dma((3,))],
        compiler_params=pltpu.CompilerParams(vmem_limit_bytes=4 << 20),
    )(*[pltpu.with_memory_space_constraint(g, vmem) for g in grads])


def solution(mesh):
    rows = P("seq", "head")
    return jax.shard_map(
        shards,
        mesh=mesh,
        in_specs=(rows, rows, rows, rows, P("head"), P("head"), P(), P("seq")),
        out_specs=(rows, rows, rows),
        check_vma=False,
    )
```

```python
import functools

import jax
import jax.numpy as jnp
from jax import lax
from jax.experimental import pallas as pl
from jax.experimental.pallas import tpu as pltpu
from jax.sharding import PartitionSpec as P

HEAD = 128
GROUP = 128
RING = 4
CHUNK = 4
UNROLL = 8
STEPS = 16
EPSILON = 1e-06
MESH = pl.DeviceIdType.MESH
F32 = jnp.float32
BF16 = jnp.bfloat16
I32 = jnp.int32
NN = ((1,), (0,))
NT = ((1,), (1,))
TN = ((0,), (0,))


def dot(a, b, dims):
    return lax.dot_general(a, b, (dims, ((), ())), preferred_element_type=F32)


def cols_of(h):
    return slice(h * HEAD, (h + 1) * HEAD)


def iota(shape, dim):
    return lax.broadcasted_iota(I32, shape, dim)


def torus_offsets(ring):
    offsets = [(dy, dz) for dy in range(ring) for dz in range(ring) if (dy, dz) != (0, 0)]
    return sorted(offsets, key=lambda o: min(o[0], ring - o[0]) + min(o[1], ring - o[1]))


def wait_bytes(ref, sem):
    pltpu.make_async_copy(ref, ref, sem).wait()


def fused_kernel(
    heads, groups, devices, sides, docs,
    rate_hbm, len_hbm, home_hbm, gain_hbm, q_hbm, k_hbm, v_hbm, u_hbm,
    qout_ref, kout_ref, vout_ref,
    rate_ref, len_ref, home_ref, gain_ref, arg_sem,
    q_ref, k_ref, v_ref, u_ref, send_ref, got1a_ref, got1b_ref, got2a_ref, got2b_ref, seq_ref, back_ref, prev_ref, after_ref,
    att_ref, vgp_ref, mix_ref,
    dec_ref, qdec_ref, kdec_ref, segr_ref, bef_ref, last_ref, segc_ref,
    hmine_ref, hall_ref, hcomp_ref, order_ref, carry_ref, homes_s, order_s, carry_s,
    mine_ref, gsum_ref,
    kv_sem, qu_sem, own_sem, smem_sem, hsend, hrecv, send1, recv1, send2, recv2a, recv2b,
    send3, recv3, send4, recv4a, recv4b, ssend, srecv,
):
    me = lax.axis_index("seq")
    side = lax.axis_index("head")
    y, z = me // RING, lax.rem(me, RING)
    flip = 1 + 2 * lax.rem(side, 2)
    peers = [
        lax.rem(y + dy * flip, RING) * RING + lax.rem(z + dz * flip, RING) for dy, dz in torus_offsets(RING)
    ]
    mates = [lax.rem(side + n, sides) for n in range(1, sides)]
    got1_ref, got2_ref = (got1a_ref, got1b_ref), (got2a_ref, got2b_ref)
    others = devices - 1
    total = devices * groups
    chunks = groups // CHUNK
    slab = CHUNK * GROUP
    part = HEAD // RING // 2

    small = [
        pltpu.make_async_copy(src, dst, arg_sem.at[n])
        for n, (src, dst) in enumerate(
            [(rate_hbm, rate_ref), (len_hbm, len_ref), (home_hbm, home_ref), (gain_hbm, gain_ref)]
        )
    ]
    for copy in small:
        copy.start()
    barrier = pltpu.get_barrier_semaphore()
    for peer in peers:
        pl.semaphore_signal(barrier, inc=1, device_id=(peer, side), device_id_type=MESH)
    for mate in mates:
        pl.semaphore_signal(barrier, inc=1, device_id=(me, mate), device_id_type=MESH)

    def slab_copy(hbm, ref, c, sem):
        rows = pl.ds(c * slab, slab)
        return pltpu.make_async_copy(hbm.at[rows], ref.at[rows], sem)

    for c in range(chunks):
        slab_copy(k_hbm, k_ref, c, kv_sem.at[0, c]).start()
        slab_copy(v_hbm, v_ref, c, kv_sem.at[1, c]).start()
    load_q = pltpu.make_async_copy(q_hbm, q_ref, qu_sem.at[0])
    load_u = pltpu.make_async_copy(u_hbm, u_ref, qu_sem.at[1])

    for copy in small:
        copy.wait()
    row = iota((GROUP, GROUP), 0).astype(F32)
    for h in range(heads):
        kdec_ref[h] = jnp.exp(-rate_ref[h] * (GROUP - 1.0 - row))

    home_rows = jnp.zeros((groups, HEAD), I32)
    home_lanes = jnp.zeros((8, HEAD), I32)
    group_row = iota((groups, HEAD), 0)
    lane8 = iota((8, HEAD), 1)
    for i in range(groups):
        home_rows = jnp.where(group_row == i, home_ref[i], home_rows)
        home_lanes = jnp.where(lane8 == i, home_ref[i], home_lanes)
    hmine_ref[...] = home_lanes
    hall_ref[me] = home_lanes
    steps = iota((8, HEAD), 0) * HEAD + lane8
    pos = home_rows * GROUP + iota((groups, HEAD), 1)
    pos_b = home_rows * GROUP - 1
    step_b = steps * GROUP - 1
    seg = jnp.zeros_like(pos)
    seg_b = jnp.zeros_like(pos)
    step_seg_b = jnp.zeros_like(steps)
    step_seg_e = jnp.zeros_like(steps)
    end = jnp.int32(0)
    for n in range(docs):
        end = end + len_ref[n]
        seg += (pos >= end).astype(I32)
        seg_b += (pos_b >= end).astype(I32)
        step_seg_b += (step_b >= end).astype(I32)
        step_seg_e += (step_b + GROUP >= end).astype(I32)
    seg_b = jnp.where(home_rows == 0, -1, seg_b).astype(F32)
    seg = seg.astype(F32)
    for i in range(groups):
        segr_ref[i] = seg[i : i + 1]
        bef_ref[i] = seg_b[i : i + 1]
        last_ref[i] = jnp.broadcast_to(seg[i : i + 1, GROUP - 1 :], (1, HEAD))
    own_rate = rate_ref[me // RING]
    keep = jnp.exp(jnp.zeros((8, HEAD), F32) - own_rate * GROUP)
    joined = (step_seg_b == step_seg_e) | (steps == 0)
    carry_ref[...] = jnp.where(joined, keep, 0.0)
    carry_copy = pltpu.make_async_copy(carry_ref, carry_s, smem_sem.at[0])
    carry_copy.start()

    def rows_of(i):
        return pl.ds(pl.multiple_of(i * GROUP, GROUP), GROUP)

    def scatter(got_ref, half, c, send_sem, recv_sem):
        for peer in peers:
            pltpu.make_async_remote_copy(
                src_ref=send_ref.at[half, peer, pl.ds(c * CHUNK, CHUNK)],
                dst_ref=got_ref[half].at[pl.ds(me * groups + c * CHUNK, CHUNK)],
                send_sem=send_sem, recv_sem=recv_sem.at[half],
                device_id=(peer, side), device_id_type=MESH,
            ).start()

    def give_back(dst_ref, half, start, size, send_sem, recv_sem):
        for peer in peers:
            pltpu.make_async_remote_copy(
                src_ref=back_ref.at[half, pl.ds(peer * groups + start, size)],
                dst_ref=dst_ref.at[half, me, pl.ds(start, size)],
                send_sem=send_sem, recv_sem=recv_sem,
                device_id=(peer, side), device_id_type=MESH,
            ).start()

    def own_slice(got_ref, half, n):
        return pltpu.make_async_copy(
            send_ref.at[half, me], got_ref[half].at[pl.ds(me * groups, groups)], own_sem.at[n, half]
        )

    def own_back(dst_ref, half, n):
        return pltpu.make_async_copy(
            back_ref.at[half, pl.ds(me * groups, groups)], dst_ref.at[half, me], own_sem.at[n, half]
        )

    def store_state(i, h, s):
        send_ref[:, RING * h : RING * (h + 1), i] = s.astype(BF16).reshape(2, RING, part, HEAD)

    def state_of(ref, i, h):
        return ref[:, RING * h : RING * (h + 1), i].reshape(HEAD, HEAD)

    def summary_group(i, _):
        rows = rows_of(i)
        seg_c = jnp.broadcast_to(segr_ref[i], (GROUP, GROUP)).T
        segc_ref[i] = seg_c
        live = seg_c == last_ref[i]
        for h in range(heads):
            cols = cols_of(h)
            w = (jnp.where(live, kdec_ref[h], 0.0) * v_ref[rows, cols].astype(F32)).astype(BF16)
            store_state(i, h, dot(k_ref[rows, cols], w, TN))
        return 0

    def summarize(c):
        slab_copy(k_hbm, k_ref, c, kv_sem.at[0, c]).wait()
        slab_copy(v_hbm, v_ref, c, kv_sem.at[1, c]).wait()
        lax.fori_loop(c * CHUNK, (c + 1) * CHUNK, summary_group, 0)

    def summary_chunk(c, _):
        summarize(c)
        scatter(got1_ref, 0, c, send1, recv1)
        return 0

    slab_copy(k_hbm, k_ref, 0, kv_sem.at[0, 0]).wait()
    slab_copy(v_hbm, v_ref, 0, kv_sem.at[1, 0]).wait()
    first = CHUNK // 2
    lax.fori_loop(0, first, summary_group, 0)
    pl.semaphore_wait(barrier, others + sides - 1)

    def first_piece(n, _):
        for peer in peers:
            pltpu.make_async_remote_copy(
                src_ref=send_ref.at[0, peer, pl.ds(n * first, first)],
                dst_ref=got1_ref[0].at[pl.ds(me * groups + n * first, first)],
                send_sem=send1, recv_sem=recv1.at[0],
                device_id=(peer, side), device_id_type=MESH,
            ).start()
        lax.fori_loop((n + 1) * first, (n + 2) * first * (1 - n), summary_group, 0)
        return 0

    lax.fori_loop(0, 2, first_piece, 0)
    load_q.start()
    load_u.start()
    for peer in peers:
        pltpu.make_async_remote_copy(
            src_ref=hmine_ref, dst_ref=hall_ref.at[me], send_sem=hsend, recv_sem=hrecv,
            device_id=(peer, side), device_id_type=MESH,
        ).start()
    lax.fori_loop(1, chunks, summary_chunk, 0)

    def second_half(c, _):
        scatter(got1_ref, 1, c, send1, recv1)
        return 0

    lax.fori_loop(0, chunks, second_half, 0)
    own_slice(got1_ref, 0, 0).start()
    own_slice(got1_ref, 1, 0).start()

    spread = row - iota((GROUP, GROUP), 1).astype(F32)
    for h in range(heads):
        r = rate_ref[h]
        dec_ref[h] = jnp.where(spread >= 0.0, jnp.exp(-r * jnp.maximum(spread, 0.0)), 0.0)
        qdec_ref[h] = jnp.exp(-r * (row + 1.0))

    wait_bytes(hall_ref.at[pl.ds(0, others)], hrecv)
    for d in range(devices):
        hcomp_ref[d : d + 1] = hall_ref[d, 0:1]
    homes_copy = pltpu.make_async_copy(hcomp_ref, homes_s, smem_sem.at[1])
    homes_copy.start()
    homes_copy.wait()

    def invert(b, acc):
        for n in range(UNROLL):
            p = b * UNROLL + n
            acc = jnp.where(steps == homes_s[p // groups, lax.rem(p, groups)], p, acc)
        return acc

    order_ref[...] = lax.fori_loop(0, total // UNROLL, invert, jnp.zeros((8, HEAD), I32))
    order_copy = pltpu.make_async_copy(order_ref, order_s, smem_sem.at[2])
    order_copy.start()
    load_q.wait()
    load_u.wait()

    def inner_group(i, _):
        rows = rows_of(i)
        same = segc_ref[i] == segr_ref[i]
        for h in range(heads):
            cols = cols_of(h)
            scores = dot(q_ref[rows, cols], k_ref[rows, cols], NT)
            mixing = (scores * jnp.where(same, dec_ref[h], 0.0)).astype(BF16)
            mix_ref[i * heads + h] = mixing
            att_ref[rows, cols] = dot(mixing, v_ref[rows, cols], NN)
        return 0

    lax.fori_loop(0, groups, inner_group, 0)
    order_copy.wait()
    carry_copy.wait()

    def scan(got_ref, half, reverse):
        def step(b, state):
            base = (total // STEPS - 1 - b if reverse else b) * STEPS
            hi, lo = base // HEAD, lax.rem(base, HEAD)
            arrived = [got_ref[half][order_s[hi, lo + n]] for n in range(STEPS)]
            keeps = [carry_s[hi, lo + n] for n in range(STEPS)]
            states = [None] * STEPS
            for n in range(STEPS):
                n = STEPS - 1 - n if reverse else n
                states[n] = state.astype(BF16)
                state = keeps[n] * state + arrived[n].astype(F32)
            for n in range(STEPS):
                seq_ref[base + n] = states[n]
            return state

        lax.fori_loop(0, total // STEPS, step, jnp.zeros((part, HEAD), F32))

        def put(d, _):
            found = [seq_ref[homes_s[d, n]] for n in range(groups)]
            for n in range(groups):
                back_ref[half, d * groups + n] = found[n]
            return 0

        lax.fori_loop(0, devices, put, 0)

    half_groups = groups // 2
    piece = CHUNK // 2

    def turn(got_ref, dst_ref, n, reverse, recv_sem, send_back, recv_first, recv_second):
        own_slice(got_ref, 0, n).wait()
        wait_bytes(got_ref[0].at[pl.ds(0, others * groups)], recv_sem.at[0])
        scan(got_ref, 0, reverse)
        give_back(dst_ref, 0, 0, half_groups, send_back, recv_first.at[0])
        own_back(dst_ref, 0, n + 1).start()
        own_slice(got_ref, 1, n).wait()
        wait_bytes(got_ref[1].at[pl.ds(0, others * groups)], recv_sem.at[1])
        scan(got_ref, 1, reverse)
        own_back(dst_ref, 1, n + 1).start()

        def rest(c, _):
            @pl.when(c == chunks // 2)
            def _():
                give_back(dst_ref, 0, half_groups, half_groups, send_back, recv_first.at[1])

            give_back(dst_ref, 1, c * CHUNK, CHUNK, send_back, recv_second.at[c])
            return 0

        lax.fori_loop(0, chunks - 1, rest, 0)
        for n in range(2):
            give_back(dst_ref, 1, groups - CHUNK + n * piece, piece, send_back, recv_second.at[chunks - 1 + n])

    def turned(dst_ref, c, recv_first, recv_second):
        @pl.when(lax.rem(c, chunks // 2) == 0)
        def _():
            wait_bytes(
                dst_ref.at[0, pl.ds(0, others), pl.ds(0, half_groups)], recv_first.at[c // (chunks // 2)]
            )

        @pl.when(c < chunks - 1)
        def _():
            wait_bytes(dst_ref.at[1, pl.ds(0, others), pl.ds(0, CHUNK)], recv_second.at[c])

    def turned_piece(dst_ref, n, recv_second):
        wait_bytes(dst_ref.at[1, pl.ds(0, others), pl.ds(0, piece)], recv_second.at[chunks - 1 + n])

    def sent(sem):
        wait_bytes(send_ref.at[0, pl.ds(0, others)], sem)
        wait_bytes(send_ref.at[0, pl.ds(0, others)], sem)

    turn(got1_ref, prev_ref, 0, False, recv1, send2, recv2a, recv2b)
    sent(send1)
    wait_bytes(hall_ref.at[pl.ds(0, others)], hsend)
    own_back(prev_ref, 0, 1).wait()
    own_back(prev_ref, 1, 1).wait()

    lane = iota((GROUP, HEAD), 1)
    pieces = GROUP // (2 * CHUNK)
    width = 2 * CHUNK

    def output_group(c, g, acc):
        i = c * CHUNK + g
        rows = rows_of(i)
        live = segc_ref[i] == bef_ref[i]
        squares = jnp.zeros((GROUP, HEAD), F32)
        crossed = jnp.zeros((GROUP, HEAD), F32)
        for h in range(heads):
            cols = cols_of(h)
            carried = dot(q_ref[rows, cols], state_of(prev_ref, i, h), NN)
            out = att_ref[rows, cols] + jnp.where(live, qdec_ref[h], 0.0) * carried
            att_ref[rows, cols] = out
            squares += out * out
            crossed += gain_ref[:, cols] * u_ref[rows, cols].astype(F32) * out
        squares = jnp.sum(squares, axis=1, keepdims=True)
        crossed = jnp.sum(crossed, axis=1, keepdims=True)
        return jnp.where(lane == g, squares, jnp.where(lane == g + CHUNK, crossed, acc))

    def total_copy(c, n):
        return pltpu.make_async_remote_copy(
            src_ref=mine_ref.at[c], dst_ref=gsum_ref.at[c, n], send_sem=ssend.at[c], recv_sem=srecv.at[c],
            device_id=(me, mates[n]), device_id_type=MESH,
        )

    def output_chunk(c):
        turned(prev_ref, c, recv2a, recv2b)

        @pl.when(c == chunks - 1)
        def _():
            turned_piece(prev_ref, 0, recv2b)
            turned_piece(prev_ref, 1, recv2b)

        acc = lax.fori_loop(0, CHUNK, functools.partial(output_group, c), jnp.zeros((GROUP, HEAD), F32))
        packed = acc[0:width]
        for n in range(1, pieces):
            packed += pltpu.roll(acc[n * width : (n + 1) * width], n * width, 1)
        mine_ref[c] = packed
        for n in range(sides - 1):
            total_copy(c, n).start()

    channels = heads * HEAD * sides

    def cotangent_group(c, sums, g, _):
        i = c * CHUNK + g
        rows = rows_of(i)
        live = segc_ref[i] == bef_ref[i]
        squares = jnp.sum(jnp.where(lane == g, sums, 0.0), axis=1, keepdims=True)
        crossed = jnp.sum(jnp.where(lane == g + CHUNK, sums, 0.0), axis=1, keepdims=True)
        scaling = lax.rsqrt(squares / channels + EPSILON)
        pull = scaling * scaling * scaling * (crossed / channels)
        for h in range(heads):
            cols = cols_of(h)
            wide = gain_ref[:, cols] * u_ref[rows, cols].astype(F32)
            grad = (scaling * wide - pull * att_ref[rows, cols]).astype(BF16)
            u_ref[rows, cols] = grad
            w = (jnp.where(live, qdec_ref[h], 0.0) * grad.astype(F32)).astype(BF16)
            store_state(i, h, dot(q_ref[rows, cols], w, TN))
        return 0

    def cotangent_chunk(c):
        wait_bytes(gsum_ref.at[c], srecv.at[c])
        wait_bytes(gsum_ref.at[c], ssend.at[c])
        both = mine_ref[c]
        for n in range(sides - 1):
            both += gsum_ref[c, n]
        sums = jnp.concatenate(
            [both] + [pltpu.roll(both, HEAD - n * width, 1) for n in range(1, pieces)], axis=0
        )
        lax.fori_loop(0, CHUNK, functools.partial(cotangent_group, c, sums), 0)
        scatter(got2_ref, 0, c, send3, recv3)

        @pl.when(c < chunks - 2)
        def _():
            scatter(got2_ref, 1, c, send3, recv3)

    def middle(c, _):
        @pl.when(c < chunks)
        def _():
            output_chunk(c)

        @pl.when(c >= 1)
        def _():
            cotangent_chunk(c - 1)

        return 0

    lax.fori_loop(0, chunks + 1, middle, 0)
    for c in (chunks - 2, chunks - 1):
        scatter(got2_ref, 1, c, send3, recv3)
    own_slice(got2_ref, 0, 2).start()
    own_slice(got2_ref, 1, 2).start()

    def local_group(i, _):
        rows = rows_of(i)
        seg_c = segc_ref[i]
        same = seg_c == segr_ref[i]
        live = seg_c == bef_ref[i]
        for h in range(heads):
            cols = cols_of(h)
            g, k, q = u_ref[rows, cols], k_ref[rows, cols], q_ref[rows, cols]
            score = (dot(g, v_ref[rows, cols], NT) * jnp.where(same, dec_ref[h], 0.0)).astype(BF16)
            carried = jnp.where(live, qdec_ref[h], 0.0) * dot(g, state_of(prev_ref, i, h), NT)
            qout_ref[rows, cols] = (dot(score, k, NN) + carried).astype(BF16)
            att_ref[rows, cols] = dot(score, q, TN)
            vgp_ref[rows, cols] = dot(mix_ref[i * heads + h], g, TN)
        return 0

    early = groups * 3 // 8
    lax.fori_loop(0, early, local_group, 0)
    sent(send2)
    turn(got2_ref, after_ref, 2, True, recv3, send4, recv4a, recv4b)
    lax.fori_loop(early, groups, local_group, 0)
    own_back(after_ref, 0, 3).wait()
    own_back(after_ref, 1, 3).wait()

    def final_group(i, _):
        rows = rows_of(i)
        live = segc_ref[i] == last_ref[i]
        for h in range(heads):
            cols = cols_of(h)
            after = state_of(after_ref, i, h)
            w = jnp.where(live, kdec_ref[h], 0.0)
            kout_ref[rows, cols] = (att_ref[rows, cols] + w * dot(v_ref[rows, cols], after, NT)).astype(BF16)
            vout_ref[rows, cols] = (vgp_ref[rows, cols] + w * dot(k_ref[rows, cols], after, NN)).astype(BF16)
        return 0

    def final_chunk(c, _):
        turned(after_ref, c, recv4a, recv4b)
        lax.fori_loop(c * CHUNK, (c + 1) * CHUNK, final_group, 0)
        return 0

    lax.fori_loop(0, chunks - 1, final_chunk, 0)
    for n in range(2):
        turned_piece(after_ref, n, recv4b)
        start = groups - CHUNK + n * piece
        lax.fori_loop(start, start + piece, final_group, 0)
    sent(send3)
    sent(send4)


def store_kernel(a_ref, b_ref, c_ref, ao_ref, bo_ref, co_ref, sem):
    pairs = ((a_ref, ao_ref), (b_ref, bo_ref), (c_ref, co_ref))
    copies = [pltpu.make_async_copy(src, dst, sem.at[n]) for n, (src, dst) in enumerate(pairs)]
    for copy in copies:
        copy.start()
    for copy in copies:
        copy.wait()


def shards(q, k, v, u, gain, rate, lengths, home):
    devices = lax.axis_size("seq")
    sides = lax.axis_size("head")
    heads = q.shape[1] // HEAD
    groups = home.shape[0]
    rows, width = q.shape
    docs = lengths.shape[0]
    total = devices * groups
    chunks = groups // CHUNK
    part = HEAD // RING // 2
    any_ = pl.BlockSpec(memory_space=pl.ANY)
    vmem, dma = pltpu.VMEM, pltpu.SemaphoreType.DMA
    table = vmem((heads, GROUP, GROUP), F32)
    strip = vmem((groups, 1, HEAD), F32)
    token = vmem((rows, width), BF16)
    flat = vmem((total, part, HEAD), BF16)
    state = vmem((2, devices, groups, part, HEAD), BF16)
    wide = vmem((rows, width), F32)
    scratch = (
        [pltpu.SMEM((heads,), F32), pltpu.SMEM((docs,), I32), pltpu.SMEM((groups,), I32)]
        + [vmem((1, width), F32), dma((4,))]
        + [token] * 4 + [state] + [flat] * 5 + [vmem((2, total, part, HEAD), BF16), state, state]
        + [wide, wide, vmem((groups * heads, GROUP, GROUP), BF16)]
        + [table] * 3 + [strip] * 3 + [vmem((groups, GROUP, GROUP), F32)]
        + [vmem((8, HEAD), I32), vmem((devices, 8, HEAD), I32), vmem((devices, HEAD), I32)]
        + [vmem((8, HEAD), I32), vmem((8, HEAD), F32)]
        + [pltpu.SMEM((devices, HEAD), I32), pltpu.SMEM((8, HEAD), I32), pltpu.SMEM((8, HEAD), F32)]
        + [vmem((chunks, 2 * CHUNK, HEAD), F32), vmem((chunks, sides - 1, 2 * CHUNK, HEAD), F32)]
        + [dma((2, chunks)), dma((2,)), dma((4, 2)), dma((3,)), dma, dma]
        + [dma, dma((2,)), dma, dma((2,)), dma((chunks + 1,))] * 2
        + [dma((chunks,)), dma((chunks,))]
    )
    grads = pl.pallas_call(
        functools.partial(fused_kernel, heads, groups, devices, sides, docs),
        out_shape=(pltpu.VMEM((rows, width), BF16),) * 3,
        in_specs=[any_] * 8,
        out_specs=(pl.BlockSpec(memory_space=vmem),) * 3,
        scratch_shapes=scratch,
        compiler_params=pltpu.CompilerParams(
            collective_id=0, has_side_effects=True, vmem_limit_bytes=50 << 20
        ),
    )(rate, lengths, home, gain.reshape(1, width), q, k, v, u)
    return pl.pallas_call(
        store_kernel,
        out_shape=(jax.ShapeDtypeStruct((rows, width), BF16),) * 3,
        in_specs=[pl.BlockSpec(memory_space=vmem)] * 3,
        out_specs=(any_,) * 3,
        scratch_shapes=[dma((3,))],
        compiler_params=pltpu.CompilerParams(vmem_limit_bytes=4 << 20),
    )(*[pltpu.with_memory_space_constraint(g, vmem) for g in grads])


def solution(mesh):
    rows = P("seq", "head")
    return jax.shard_map(
        shards,
        mesh=mesh,
        in_specs=(rows, rows, rows, rows, P("head"), P("head"), P(), P("seq")),
        out_specs=(rows, rows, rows),
        check_vma=False,
    )
```
